512 devices in a mesh: dom: 128 (over z, x, core), rep: 4 (over y).
Axes of the slice: x: 4, y: 4, z: 16, core: 2. Of those that a mesh axis runs over, the one named last changes fastest.
Arguments:
- features: bfloat16 [32768, 256], P('dom'), may hold values from -6 to 6
- positions: float32 [3, 32768], P(None, 'dom'), may hold values from -6 to 6
- radial: bfloat16 [8, 256, 256], replicated, may hold values from -0.03125 to 0.03125
- mixing: bfloat16 [256, 256], replicated, may hold values from -0.375 to 0.375
- readout: float32 [256], replicated, may hold values from -4 to 4
- decay: float32 [8], replicated, may hold values from 0.1 to 1
- send_rows: int32 [4, 16384], P(None, 'dom'), may hold values from 0 to 255
- pair_home: int32 [24576], P(('dom', 'rep')), may hold values from 0 to 1
- pair_other: int32 [24576], P(('dom', 'rep')), may hold values from 0 to 5
- pair_kind: int32 [24576], P(('dom', 'rep')), may hold values from 0 to 7
- pair_image: int32 [3, 24576], P(None, ('dom', 'rep')), may hold values from -1 to 1
Outputs:
- grad_features: bfloat16 [32768, 256], P('dom')
- forces: float32 [3, 32768], P(None, 'dom')
- virials: float32 [6, 32768], P(None, 'dom')
- grad_mixing: float32 [256, 256], P('dom', 'rep')
The draws below stay inside these ranges and needn't reach their ends.
Inputs may be any that keep to these rules, and one draw needn't show every extreme that they name: `send_rows`: rows may repeat within a round.
All inputs are finite; a program needn't handle non-finite values.
Results may differ from the reference program's by a relative error of at most 0.006.
Values may be sent and summed in bfloat16 or wider, within the bound.
No kernel may reach another device: no remote copies, remote signals or barrier semaphores. Data moves between devices by JAX's collectives and lax.ppermute only.
A program may use at most 128 MiB of HBM per device.

```python
import math
import jax
import jax.numpy as jnp
from jax import lax

C = 256
RADIAL = 8
TILE_ATOMS = 128
ROUNDS = 4
SUBDOMAIN_ATOMS = 256
PAIRS_DEV = 48
NATOM = 32768
PAIRS = 24576
N_DOM = 128
N_REP = 4


def plant(array, key, smallest, top_value):
    place = [jax.random.randint(jax.random.fold_in(key, axis), (), 0, length) for axis, length in enumerate(array.shape)]
    widest = array.shape.index(max(array.shape))
    next_to = place[:widest] + [(place[widest] + 1) % array.shape[widest]] + place[widest + 1:]
    return array.at[tuple(place)].set(smallest).at[tuple(next_to)].set(top_value)


def steps_of(own_key, extent, cuts, least, top_value):
    def one(position, blocks):
        steps = jax.random.uniform(jax.random.fold_in(jax.random.fold_in(own_key, 6), position), (blocks,), jnp.float32, least / len(cuts), top_value / len(cuts))
        return jnp.repeat(jnp.exp(steps), extent[position] // blocks).reshape((-1,) + (1,) * (len(extent) - position - 1))

    level = one(*cuts[0])
    for cut in cuts[1:]:
        level = level * one(*cut)
    return level


def scatter_about(own_key, dims, spread, bound, split=(), dtype=jnp.bfloat16):
    loudness = steps_of(own_key, dims, split, -0.22, 0.18) if split else 1.0
    entries = jax.random.normal(own_key, dims, jnp.float32) * spread * loudness
    return jnp.minimum(jnp.maximum(entries, -bound), bound).astype(dtype)


def setup_inputs(seed: int = 0) -> dict:
    arg_keys = jax.random.split(jax.random.key(seed), 12)
    return {
        "features": scatter_about(arg_keys[0], (NATOM, C), 1.0, 6.0, ((0, 128),)),
        "positions": scatter_about(arg_keys[1], (3, NATOM), 1.0, 6.0, ((1, 128),), jnp.float32),
        "radial": scatter_about(arg_keys[2], (RADIAL, C, C), (C * TILE_ATOMS) ** -0.5, 0.03125),
        "mixing": scatter_about(arg_keys[3], (C, C), C ** -0.5, 0.375),
        "readout": scatter_about(arg_keys[4], (C,), 1.0, 4.0, (), jnp.float32),
        "decay": jnp.clip(jnp.exp(jax.random.uniform(arg_keys[5], (RADIAL,), jnp.float32, math.log(0.1), math.log(1.0))), 0.1, 1.0),
        "send_rows": plant(jax.random.randint(arg_keys[6], (ROUNDS, TILE_ATOMS * N_DOM), 0, SUBDOMAIN_ATOMS), jax.random.fold_in(arg_keys[6], 1), 0, SUBDOMAIN_ATOMS - 1).astype(jnp.int32),
        "pair_home": plant(jax.random.randint(arg_keys[7], (PAIRS,), 0, SUBDOMAIN_ATOMS // TILE_ATOMS), jax.random.fold_in(arg_keys[7], 1), 0, (SUBDOMAIN_ATOMS // TILE_ATOMS) - 1).astype(jnp.int32),
        "pair_other": plant(jax.random.randint(arg_keys[8], (PAIRS,), 0, SUBDOMAIN_ATOMS // TILE_ATOMS + ROUNDS), jax.random.fold_in(arg_keys[8], 1), 0, (SUBDOMAIN_ATOMS // TILE_ATOMS + ROUNDS) - 1).astype(jnp.int32),
        "pair_kind": plant(jax.random.randint(arg_keys[9], (PAIRS,), 0, RADIAL), jax.random.fold_in(arg_keys[9], 1), 0, RADIAL - 1).astype(jnp.int32),
        "pair_image": plant(jax.random.randint(arg_keys[10], (3, PAIRS), -1, 2), jax.random.fold_in(arg_keys[10], 1), -1, 1).astype(jnp.int32),
    }


offsets = (1, -1, 2, -2)
cell_edge = 2.0
component_pairs = ((0, 0), (1, 1), (2, 2), (0, 1), (0, 2), (1, 2))
highest_precision = lax.Precision.HIGHEST


def lowered(values):
    return lax.optimization_barrier(values.astype(jnp.bfloat16)).astype(jnp.float32)


def pair_setup(ext_feat, ext_pos, home_tile, other_tile, radial_pick, image_shift, radial, decay):
    tiles_feat = ext_feat.reshape(-1, TILE_ATOMS, ext_feat.shape[1])
    tiles_pos = ext_pos.reshape(3, -1, TILE_ATOMS)
    far_end = jnp.take(tiles_pos, other_tile, axis=1) + image_shift[:, :, None].astype(jnp.float32) * cell_edge
    near_end = jnp.take(tiles_pos, home_tile, axis=1)
    separation = far_end[:, :, None, :] - near_end[:, :, :, None]
    rates = jnp.take(decay, radial_pick)
    kernel = jnp.exp(-rates[:, None, None] * jnp.sum(separation * separation, axis=0))
    partner_rows = jnp.take(tiles_feat, other_tile, axis=0).astype(jnp.float32)
    chosen = jnp.take(radial, radial_pick, axis=0).astype(jnp.float32)
    mapped = lowered(jnp.einsum('pbc,pcd->pbd', partner_rows, chosen, precision=highest_precision))
    return separation, rates, kernel, mapped, chosen


def reference(features, positions, radial, mixing, readout, decay, send_rows, pair_home, pair_other, pair_kind, pair_image):
    channel_count = features.shape[1]
    home_tiles = SUBDOMAIN_ATOMS // TILE_ATOMS
    extended_tiles = home_tiles + ROUNDS
    pair_count = PAIRS_DEV * N_REP
    domain_feat = features.reshape(N_DOM, SUBDOMAIN_ATOMS, channel_count)
    domain_pos = positions.reshape(3, N_DOM, SUBDOMAIN_ATOMS).transpose(1, 0, 2)
    send_table = send_rows.reshape(ROUNDS, N_DOM, TILE_ATOMS)
    halo_feat = []
    halo_pos = []
    for section_no in range(ROUNDS):
        picked_feat = jnp.take_along_axis(domain_feat, send_table[section_no][:, :, None], axis=1)
        picked_pos = jnp.take_along_axis(domain_pos, send_table[section_no][:, None, :], axis=2)
        halo_feat.append(jnp.roll(picked_feat, offsets[section_no], axis=0))
        halo_pos.append(jnp.roll(picked_pos, offsets[section_no], axis=0))
    ext_feat = jnp.concatenate([domain_feat] + halo_feat, axis=1)
    ext_pos = jnp.concatenate([domain_pos] + halo_pos, axis=2)
    home_tile = pair_home.reshape(N_DOM, pair_count)
    other_tile = pair_other.reshape(N_DOM, pair_count)
    radial_pick = pair_kind.reshape(N_DOM, pair_count)
    image_shift = pair_image.reshape(3, N_DOM, pair_count).transpose(1, 0, 2)
    home_iota = lax.iota(jnp.int32, home_tiles)
    ext_iota = lax.iota(jnp.int32, extended_tiles)

    def forward_domain(inputs):
        feat_one, pos_one, home_one, other_one, pick_one, shift_one = inputs
        separation, rates, kernel, mapped, chosen = pair_setup(feat_one, pos_one, home_one, other_one, pick_one, shift_one, radial, decay)
        message_rows = jnp.einsum('pab,pbd->pad', lowered(kernel), mapped, precision=highest_precision)
        home_lookup_table = (home_one[None, :] == home_iota[:, None]).astype(jnp.float32)
        return jnp.einsum('so,oxe->sxe', home_lookup_table, message_rows, precision=highest_precision).reshape(SUBDOMAIN_ATOMS, channel_count)

    message = lax.map(forward_domain, (ext_feat, ext_pos, home_tile, other_tile, radial_pick, image_shift))
    message = message.reshape(NATOM, channel_count)
    packed = message.astype(jnp.bfloat16)
    mixed_rows = jnp.dot(packed, mixing, preferred_element_type=jnp.float32)
    sigmoid_rows = jax.nn.sigmoid(mixed_rows)
    slope_rows = (readout * sigmoid_rows * (1.0 + mixed_rows * (1.0 - sigmoid_rows))).astype(jnp.bfloat16)
    adjoint = jnp.dot(slope_rows, mixing.T, preferred_element_type=jnp.float32).astype(jnp.bfloat16)
    grad_mixing = jnp.dot(packed.T, slope_rows, preferred_element_type=jnp.float32)
    adjoint_dom = adjoint.reshape(N_DOM, SUBDOMAIN_ATOMS, channel_count)

    def backward_domain(inputs):
        feat_one, pos_one, home_one, other_one, pick_one, shift_one, adjoint_one = inputs
        separation, rates, kernel, mapped, chosen = pair_setup(feat_one, pos_one, home_one, other_one, pick_one, shift_one, radial, decay)
        kernel_low = lowered(kernel)
        adjoint_tiles = jnp.take(adjoint_one.reshape(home_tiles, TILE_ATOMS, channel_count), home_one, axis=0).astype(jnp.float32)
        kernel_grad = jnp.einsum('pad,pbd->pab', adjoint_tiles, mapped, precision=highest_precision)
        mapped_grad = lowered(jnp.einsum('pab,pad->pbd', kernel_low, adjoint_tiles, precision=highest_precision))
        feature_grad = jnp.einsum('pbd,pcd->pbc', mapped_grad, chosen, precision=highest_precision)
        weight = -2.0 * rates[:, None, None] * kernel * kernel_grad
        home_atom_side = []
        partner_side = []
        for axis_one in range(3):
            pull = weight * separation[axis_one]
            home_atom_side.append(jnp.sum(pull, axis=2))
            partner_side.append(-jnp.sum(pull, axis=1))
        for axis_one, axis_two in component_pairs:
            product = weight * separation[axis_one] * separation[axis_two]
            home_atom_side.append(-0.5 * jnp.sum(product, axis=2))
            partner_side.append(-0.5 * jnp.sum(product, axis=1))
        home_atom_side = jnp.stack(home_atom_side)
        partner_side = jnp.stack(partner_side)
        home_lookup_table = (home_one[None, :] == home_iota[:, None]).astype(jnp.float32)
        partner_table = (other_one[None, :] == ext_iota[:, None]).astype(jnp.float32)
        ext_grad = jnp.einsum('jp,pbc->jbc', partner_table, feature_grad, precision=highest_precision).reshape(extended_tiles * TILE_ATOMS, channel_count)
        extended_side = jnp.einsum('it,ztq->ziq', partner_table, partner_side, precision=highest_precision).reshape(9, extended_tiles * TILE_ATOMS)
        self_side = jnp.einsum('qk,gkv->gqv', home_lookup_table, home_atom_side, precision=highest_precision).reshape(9, SUBDOMAIN_ATOMS) + extended_side[:, :SUBDOMAIN_ATOMS]
        return ext_grad[:SUBDOMAIN_ATOMS], self_side, ext_grad[SUBDOMAIN_ATOMS:], extended_side[:, SUBDOMAIN_ATOMS:]

    own_grad, self_side, halo_grad, halo_side = lax.map(backward_domain, (ext_feat, ext_pos, home_tile, other_tile, radial_pick, image_shift, adjoint_dom))
    atom_iota = lax.iota(jnp.int32, SUBDOMAIN_ATOMS)
    for section_no in range(ROUNDS):
        returned_grad = jnp.roll(halo_grad[:, section_no * TILE_ATOMS:(section_no + 1) * TILE_ATOMS], -offsets[section_no], axis=0)
        returned_side = jnp.roll(halo_side[:, :, section_no * TILE_ATOMS:(section_no + 1) * TILE_ATOMS], -offsets[section_no], axis=0)
        send_onehot = (send_table[section_no][:, :, None] == atom_iota[None, None, :]).astype(jnp.float32)
        own_grad = own_grad + jnp.einsum('dta,dtc->dac', send_onehot, returned_grad, precision=highest_precision)
        self_side = self_side + jnp.einsum('dta,dct->dca', send_onehot, returned_side, precision=highest_precision)
    grad_features = own_grad.reshape(NATOM, channel_count).astype(jnp.bfloat16)
    forces = self_side[:, :3].transpose(1, 0, 2).reshape(3, NATOM)
    virials = self_side[:, 3:].transpose(1, 0, 2).reshape(6, NATOM)
    return grad_features, forces, virials, grad_mixing
```

```python
import functools

import jax
import jax.numpy as jnp
from jax import lax
from jax.experimental import pallas as pl
from jax.experimental.pallas import tpu as pltpu
from jax.sharding import PartitionSpec as P

TILE = 128
SLOTS = 3
QUAD = 4
SIDE = 16
OFFSETS = (1, -1, 2, -2)
EDGE = 2.0
FAR = 1.0e4
F32, BF16, I32 = jnp.float32, jnp.bfloat16, jnp.int32
COMPONENT_PAIRS = ((0, 0), (1, 1), (2, 2), (0, 1), (0, 2), (1, 2))

NN = (((1,), (0,)), ((), ()))
NT = (((1,), (1,)), ((), ()))
TN = (((0,), (0,)), ((), ()))


def dot(a, b, dims=NN):
    return lax.dot_general(a, b, dims, preferred_element_type=F32)


def iota(shape, dim):
    return lax.broadcasted_iota(I32, shape, dim)


def ones_where(mask, dtype=BF16):
    return jnp.where(mask, 1.0, 0.0).astype(dtype)


def split(x):
    high = x.astype(BF16).astype(F32)
    return high, (x - high).astype(BF16).astype(F32)


def pack_kernel(rows, feat, pos, home, other, kind, image, send, lists, pad, block):
    rep = lax.axis_index("rep")
    atoms = feat.shape[0]
    count = home.shape[1]
    pick = ones_where(iota((atoms, TILE), 0) == rows[pl.ds(rep, 1), :])
    send[0:TILE, :] = dot(pick, feat[...], TN).astype(BF16)
    pad[...] = jnp.zeros_like(pad)
    pad[0:3, :] = pos[...]
    whole = pad[...]
    high, mid = split(whole)
    low = whole - high - mid
    parts = jnp.concatenate([high, mid, low, jnp.zeros_like(low)], axis=0).astype(BF16)
    moved = dot(parts, pick).astype(BF16)
    send[TILE : TILE + SIDE, 0:TILE] = moved[0:SIDE]
    send[TILE : TILE + SIDE, TILE : 2 * TILE] = moved[SIDE : 2 * SIDE]
    block[...] = jnp.zeros_like(block)
    for q in range(4):

        @pl.when(rep == q)
        def _(q=q):
            span = slice(q * count, (q + 1) * count)
            block[0:1, span] = home[...]
            block[1:2, span] = other[...]
            block[2:3, span] = kind[...]
            block[3:6, span] = image[...]

    for q in range(4):
        lists[8 * q : 8 * q + 8, :] = block[...]


def plan_kernel(count, lists, plan):
    rep = lax.axis_index("rep")
    lanes = lists.shape[1]
    table = lists[0:8, :] + lists[8:16, :] + lists[16:24, :] + lists[24:32, :]
    home, other = table[0:1, :], table[1:2, :]
    valid = jnp.where(iota((1, lanes), 1) < 4 * count, 1, 0)
    ahead = ones_where(iota((lanes, lanes), 0) < iota((lanes, lanes), 1))

    def before(first, second):
        both = jnp.where(iota((16, lanes), 0) < 8, first, second)
        found = dot(both.astype(F32).astype(BF16), ahead).astype(I32)
        return found[0:1, :], found[8:9, :]

    def total(x):
        return jnp.sum(x.astype(F32), axis=1, keepdims=True).astype(I32)

    local = jnp.where(other < 2, valid, 0)
    start = jnp.zeros((1, 1), I32)
    quota = jnp.zeros((1, 1), I32)
    for q in range(4):
        room = jnp.maximum(count - total(jnp.where(other == 2 + q, valid, 0)), 0)
        start = start + jnp.where(q < rep, room, 0)
        quota = quota + jnp.where(q == rep, room, 0)
    turn, _ = before(local, local)
    taken = jnp.where(turn >= start, local, 0) * jnp.where(turn < start + quota, 1, 0)
    mine = taken + jnp.where(other == 2 + rep, valid, 0)
    first = jnp.where(home == 0, mine, 0)
    second = mine - first
    place_first, place_second = before(first, second)
    quads_first = (total(first) + (QUAD - 1)) // QUAD
    quads_second = (total(second) + (QUAD - 1)) // QUAD
    place = jnp.where(first > 0, place_first, place_second + quads_first * QUAD)
    place = jnp.where(mine > 0, place, -1)
    put = ones_where(iota((lanes, lanes), 0) == place)
    row = iota((8, lanes), 0)
    fields = jnp.where(row == 1, jnp.minimum(table, 2), table)
    fields = jnp.where(row == 6, 1, fields).astype(F32)
    fields = jnp.concatenate([fields, jnp.zeros_like(fields)], axis=0).astype(BF16)
    listed = dot(fields, put, NT)[0:8, :].astype(I32)
    plan[...] = jnp.where(row == 7, quads_first + quads_second, listed)


def place_coordinates(pos, halo, rows, columns):
    rows[...] = jnp.zeros_like(rows)
    for t in range(2):
        rows[t, 0:3, :] = pos[:, t * TILE : (t + 1) * TILE]
    side = halo[TILE : TILE + SIDE, :].astype(F32)
    rows[2] = side[0:8, 0:TILE] + side[8:16, 0:TILE] + side[0:8, TILE : 2 * TILE]
    for t in range(2):
        block = rows[t]
        for c in range(3):
            columns[t * 3 + c] = jnp.transpose(jnp.broadcast_to(block[c : c + 1, :], (TILE, TILE)))


def pair_fields(plan, decay, p):
    slot, kind = plan[1, p], plan[2, p]
    shift = [plan[3 + c, p].astype(F32) * EDGE for c in range(3)]
    away = (1 - plan[6, p]).astype(F32) * FAR
    return slot, kind, shift, away, decay[kind]


def radial_kernel(rows, columns, home, slot, shift, away, rate):
    partner = rows[slot]
    square = None
    for c in range(3):
        by = shift[c] + away if c == 0 else shift[c]
        apart = (partner[c : c + 1, :] + by) - columns[home * 3 + c]
        square = apart * apart if square is None else square + apart * apart
    return jnp.exp(square * (-rate))


def tile_of(slot):
    return pl.ds(pl.multiple_of(slot * TILE, TILE), TILE)


def forward_kernel(plan, decay, feat, pos, halo, radial, mapped, partial, rows, columns, message):
    place_coordinates(pos, halo, rows, columns)
    atoms = feat.shape[0]
    for k in range(radial.shape[0]):
        mapped[k, 0:atoms, :] = dot(feat[...], radial[k]).astype(BF16)
        mapped[k, atoms : atoms + TILE, :] = dot(halo[0:TILE, :], radial[k]).astype(BF16)
    message[...] = jnp.zeros_like(message)

    def quad(q, carry):
        home = plan[0, q * QUAD]
        total = None
        for u in range(QUAD):
            slot, kind, shift, away, rate = pair_fields(plan, decay, q * QUAD + u)
            kernel = radial_kernel(rows, columns, home, slot, shift, away, rate).astype(BF16)
            part = dot(kernel, mapped[kind, tile_of(slot), :])
            total = part if total is None else total + part
        message[home] += total
        return carry

    lax.fori_loop(0, plan[7, 0], quad, 0)
    for t in range(2):
        low = message[t].astype(BF16)
        for q in range(4):
            partial[q * atoms + t * TILE : q * atoms + (t + 1) * TILE, :] = low


def backward_kernel(
    plan, decay, partial, mixing, readout, pos, halo, radial, mapped,
    back, own_grad, own_side, mixing_part,
    rows, columns, adjoint, flipped, turned, bases, sums, side,
):
    rep = lax.axis_index("rep")
    atoms, channels = own_grad.shape
    place_coordinates(pos, halo, rows, columns)
    message = partial[0:atoms, :].astype(F32)
    for q in range(1, 4):
        message = message + partial[q * atoms : (q + 1) * atoms, :].astype(F32)
    packed = message.astype(BF16)
    mixed = dot(packed, mixing[...])
    gate = jax.nn.sigmoid(mixed)
    slope = (readout[...] * gate * (1.0 + mixed * (1.0 - gate))).astype(BF16)
    adjoint[...] = dot(slope, mixing[...], NT).astype(BF16).reshape(2, TILE, channels)
    for t in range(2):
        flipped[t] = dot(mixing[...], slope[t * TILE : (t + 1) * TILE, :], NT).astype(BF16)

    half = channels // 2
    share = channels // 4
    gradient = None
    for odd in range(2):
        take_rows = ones_where(iota((channels, half), 0) == 2 * iota((channels, half), 1) + odd)
        lane = iota((channels, TILE), 1) - odd * share
        inside = jnp.where(lane >= 0, 1, 0) * jnp.where(lane < share, 1, 0)
        take_cols = ones_where(jnp.where(inside > 0, lane + rep * share, -1) == iota((channels, TILE), 0))
        left = dot(packed, take_rows).astype(BF16)
        right = dot(slope, take_cols).astype(BF16)
        part = dot(left, right, TN)
        gradient = part if gradient is None else gradient + part
    mixing_part[...] = gradient

    row = iota((SIDE, TILE), 0)

    def marks(*which):
        found = jnp.zeros((SIDE, TILE), F32)
        for r in which:
            found = jnp.where(row == r, 1.0, found)
        return found

    left_marks = (marks(1, 4, 8, 9), marks(2, 5, 10), marks(3, 6))
    right_marks = (marks(4), marks(5, 8), marks(6, 9, 10))
    left_one, right_one = marks(0), marks(0, 1, 2, 3)
    for t in range(SLOTS):
        block = rows[t]
        left, right = left_one, right_one
        for c in range(3):
            left = left + left_marks[c] * block[c : c + 1, :]
            right = right + right_marks[c] * block[c : c + 1, :]
        bases[t, 0:SIDE, :] = left
        bases[t, SIDE : 2 * SIDE, :] = right
    sums[...] = jnp.zeros_like(sums)
    turned[...] = jnp.zeros_like(turned)

    def monomials(t, left_shift, right_shift):
        base = bases[t]
        high, low = split((base[0:SIDE] + left_shift) * (base[SIDE : 2 * SIDE] + right_shift))
        both = jnp.concatenate([high, low], axis=0).astype(BF16)
        return jnp.concatenate([both, both], axis=1)

    def quad(q, carry):
        home = plan[0, q * QUAD]
        home_sum = None
        for u in range(QUAD):
            slot, kind, shift, away, rate = pair_fields(plan, decay, q * QUAD + u)
            kernel = radial_kernel(rows, columns, home, slot, shift, away, rate)
            pull = dot(adjoint[home], mapped[kind, tile_of(slot), :], NT)
            weight = (kernel * (-2.0 * rate)) * pull
            high = weight.astype(BF16)
            low = (weight - high.astype(F32)).astype(BF16)
            left_shift = sum(left_marks[c] * shift[c] for c in range(3))
            right_shift = sum(right_marks[c] * shift[c] for c in range(3))
            far = monomials(slot, left_shift, right_shift)
            near = monomials(home, -left_shift, -right_shift)
            part = dot(far, jnp.concatenate([high, low], axis=1), NT)
            home_sum = part if home_sum is None else home_sum + part
            sums[slot] += dot(near, jnp.concatenate([high, low], axis=0))
            turned[kind * SLOTS + slot] += dot(flipped[home], kernel.astype(BF16))
        sums[home] += home_sum
        return carry

    lax.fori_loop(0, plan[7, 0], quad, 0)

    side[...] = jnp.zeros_like(side)
    for t in range(SLOTS):
        found = sums[t]
        found = found[0:SIDE] + found[SIDE : 2 * SIDE]
        at = [rows[t][c : c + 1, :] for c in range(3)]
        zeroth = found[0:1, :]
        once = [found[1 + c : 2 + c, :] for c in range(3)]
        for c in range(3):
            side[t, c : c + 1, :] = once[c] - at[c] * zeroth
        for n, (a, b) in enumerate(COMPONENT_PAIRS):
            at_row = 4 + n if n < 3 else 5 + n
            twice = found[at_row : at_row + 1, :]
            side[t, 8 + n : 9 + n, :] = -0.5 * (
                twice - at[b] * once[a] - at[a] * once[b] + at[a] * at[b] * zeroth
            )
        total = None
        for k in range(radial.shape[0]):
            part = dot(radial[k], turned[k * SLOTS + t].astype(BF16))
            total = part if total is None else total + part
        gradient = jnp.transpose(total)
        if t < 2:
            own_grad[t * TILE : (t + 1) * TILE, :] = gradient
            own_side[:, t * TILE : (t + 1) * TILE] = side[t]
        else:
            back[0:TILE, :] = gradient.astype(BF16)
            high, low = split(side[t])
            back[TILE : TILE + SIDE, 0:TILE] = high.astype(BF16)
            back[TILE : TILE + SIDE, TILE : 2 * TILE] = low.astype(BF16)


def return_kernel(rows, got, own_grad, own_side, payload):
    rep = lax.axis_index("rep")
    atoms = own_grad.shape[0]
    pick = ones_where(iota((atoms, TILE), 0) == rows[pl.ds(rep, 1), :])
    grad = (own_grad[...] + dot(pick, got[0:TILE, :])).astype(BF16)
    came = got[TILE : TILE + SIDE, :]
    side = own_side[...] + dot(came[:, 0:TILE], pick, NT) + dot(came[:, TILE : 2 * TILE], pick, NT)
    high, low = split(side)
    both = jnp.concatenate([high, low], axis=0).astype(BF16)
    height = atoms + 2 * SIDE
    for q in range(4):
        payload[q * height : q * height + atoms, :] = grad
        payload[q * height + atoms : (q + 1) * height, :] = both


def final_kernel(payload, mixing_parts, grad, forces, virials, grad_mixing):
    atoms = grad.shape[0]
    height = atoms + 2 * SIDE
    total = None
    side = None
    for q in range(4):
        part = payload[q * height : q * height + atoms, :].astype(F32)
        total = part if total is None else total + part
        both = payload[q * height + atoms : (q + 1) * height, :].astype(F32)
        part = both[0:SIDE] + both[SIDE : 2 * SIDE]
        side = part if side is None else side + part
    grad[...] = total.astype(BF16)
    forces[...] = side[0:3]
    virials[...] = side[8:14]
    found = jnp.sum(mixing_parts[...], axis=0, keepdims=True)
    share = grad_mixing.shape[1]
    grad_mixing[0:1, :] = found[:, 0:share]
    grad_mixing[1:2, :] = found[:, share : 2 * share]


def call(kernel, outs, ins, scratch=(), scalars=0, flops=0, moved=1 << 20):
    vmem = pl.BlockSpec(memory_space=pltpu.VMEM)
    smem = pl.BlockSpec(memory_space=pltpu.SMEM)
    return pl.pallas_call(
        kernel,
        out_shape=[jax.ShapeDtypeStruct(shape, dtype) for shape, dtype in outs],
        in_specs=[smem] * scalars + [vmem] * (len(ins) - scalars),
        out_specs=[vmem] * len(outs),
        scratch_shapes=[pltpu.VMEM(shape, dtype) for shape, dtype in scratch],
        compiler_params=pltpu.CompilerParams(vmem_limit_bytes=40 << 20),
        cost_estimate=pl.CostEstimate(flops=flops, bytes_accessed=moved, transcendentals=0),
    )(*ins)


def on_device(
    features, positions, radial, mixing, readout, decay,
    send_rows, pair_home, pair_other, pair_kind, pair_image,
):
    atoms, channels = features.shape
    kinds = radial.shape[0]
    count = pair_home.shape[0]
    doms, reps = lax.axis_size("dom"), lax.axis_size("rep")
    lanes = 2 * TILE
    assert reps == len(OFFSETS) and atoms == 2 * TILE and 4 * count <= lanes - 64

    def hop(array, sign):
        ways = [
            (d * reps + r, (d + sign * OFFSETS[r]) % doms * reps + r)
            for d in range(doms)
            for r in range(reps)
        ]
        return lax.ppermute(array, ("dom", "rep"), ways)

    send, lists = call(
        pack_kernel,
        [((TILE + SIDE, channels), BF16), ((32, lanes), I32)],
        [send_rows, features, positions]
        + [x.reshape(1, count) for x in (pair_home, pair_other, pair_kind)]
        + [pair_image],
        [((8, atoms), F32), ((8, lanes), I32)],
        flops=1 << 24,
    )
    halo = hop(send, 1)
    lists = lax.all_to_all(lists, "rep", 0, 0, tiled=True)
    [plan] = call(functools.partial(plan_kernel, count), [((8, lanes), I32)], [lists], flops=1 << 20)

    coordinates = [((SLOTS, 8, TILE), F32), ((6, TILE, TILE), F32)]
    mapped, partial = call(
        forward_kernel,
        [((kinds, SLOTS * TILE, channels), BF16), ((reps * atoms, channels), BF16)],
        [plan, decay, features, positions, halo, radial],
        coordinates + [((2, TILE, channels), F32)],
        scalars=2,
        flops=1 << 30,
    )
    partial = lax.all_to_all(partial, "rep", 0, 0, tiled=True)
    back, own_grad, own_side, mixing_part = call(
        backward_kernel,
        [
            ((TILE + SIDE, channels), BF16),
            ((atoms, channels), F32),
            ((SIDE, atoms), F32),
            ((channels // 2, TILE), F32),
        ],
        [plan, decay, partial, mixing, readout.reshape(1, channels), positions, halo, radial, mapped],
        coordinates
        + [
            ((2, TILE, channels), BF16),
            ((2, channels, TILE), BF16),
            ((kinds * SLOTS, channels, TILE), F32),
            ((SLOTS, 2 * SIDE, TILE), F32),
            ((SLOTS, 2 * SIDE, TILE), F32),
            ((SLOTS, SIDE, TILE), F32),
        ],
        scalars=2,
        flops=1 << 31,
    )
    got = hop(back, -1)
    rows_each = channels // 2 // doms
    mixing_parts = lax.all_to_all(mixing_part, "dom", 0, 0, tiled=True)
    height = atoms + 2 * SIDE
    [payload] = call(
        return_kernel,
        [((reps * height, channels), BF16)],
        [send_rows, got, own_grad, own_side],
        flops=1 << 24,
    )
    payload = lax.all_to_all(payload, "rep", 0, 0, tiled=True)
    return tuple(
        call(
            final_kernel,
            [
                ((atoms, channels), BF16),
                ((3, atoms), F32),
                ((6, atoms), F32),
                ((2 * rows_each, channels // reps), F32),
            ],
            [payload, mixing_parts],
            flops=1 << 20,
        )
    )


def solution(mesh):
    in_specs = (
        P("dom", None),
        P(None, "dom"),
        P(),
        P(),
        P(),
        P(),
        P(None, "dom"),
        P(("dom", "rep")),
        P(("dom", "rep")),
        P(("dom", "rep")),
        P(None, ("dom", "rep")),
    )
    out_specs = (P("dom", None), P(None, "dom"), P(None, "dom"), P("dom", "rep"))
    return jax.shard_map(
        on_device, mesh=mesh, in_specs=in_specs, out_specs=out_specs, check_vma=False
    )
```

```python
import functools

import jax
import jax.numpy as jnp
from jax import lax
from jax.experimental import pallas as pl
from jax.experimental.pallas import tpu as pltpu
from jax.sharding import PartitionSpec as P

TILE = 128
SLOTS = 3
QUAD = 8
SIDE = 16
OFFSETS = (1, -1, 2, -2)
EDGE = 2.0
FAR = 1.0e4
DEPTH = 64
F32, BF16, I32 = jnp.float32, jnp.bfloat16, jnp.int32
COMPONENT_PAIRS = ((0, 0), (1, 1), (2, 2), (0, 1), (0, 2), (1, 2))

NN = (((1,), (0,)), ((), ()))
NT = (((1,), (1,)), ((), ()))
TN = (((0,), (0,)), ((), ()))


def dot(a, b, dims=NN):
    return lax.dot_general(a, b, dims, preferred_element_type=F32)


def iota(shape, dim):
    return lax.broadcasted_iota(I32, shape, dim)


def ones_where(mask, dtype=BF16):
    return jnp.where(mask, 1.0, 0.0).astype(dtype)


def split(x):
    high = x.astype(BF16).astype(F32)
    return high, (x - high).astype(BF16).astype(F32)


def split3(x):
    high, mid = split(x)
    return high, mid, x - high - mid


def fetch(sources, targets, sems):
    copies = [pltpu.make_async_copy(a, b, sems.at[n]) for n, (a, b) in enumerate(zip(sources, targets))]
    for copy in copies:
        copy.start()
    return copies


def pack_kernel(
    hbm_rows, hbm_home, hbm_other, hbm_kind, hbm_image, hbm_pos, hbm_feat,
    send, lists,
    rows, home, other, kind, image, pos, feat, block, sems,
):
    copies = fetch(
        (hbm_rows, hbm_home, hbm_other, hbm_kind, hbm_image, hbm_pos, hbm_feat),
        (rows, home, other, kind, image, pos.at[0:3, :], feat),
        sems,
    )
    rep = lax.axis_index("rep")
    atoms = feat.shape[0]
    count = home.shape[1]
    pos[3:8, :] = jnp.zeros((5, atoms), F32)
    block[...] = jnp.zeros_like(block)
    for copy in copies:
        copy.wait()
    pick = ones_where(iota((atoms, TILE), 0) == rows[pl.ds(rep, 1), :])
    send[0:TILE, :] = dot(pick, feat[...], TN).astype(BF16)
    parts = jnp.concatenate([*split3(pos[...]), jnp.zeros_like(pos)], axis=0).astype(BF16)
    moved = dot(parts, pick).astype(BF16)
    send[TILE : TILE + SIDE, 0:TILE] = moved[0:SIDE]
    send[TILE : TILE + SIDE, TILE : 2 * TILE] = moved[SIDE : 2 * SIDE]
    for q in range(4):

        @pl.when(rep == q)
        def _(q=q):
            span = slice(q * count, (q + 1) * count)
            block[0:1, span] = home[...]
            block[1:2, span] = other[...]
            block[2:3, span] = kind[...]
            block[3:6, span] = image[...]

    for q in range(4):
        lists[8 * q : 8 * q + 8, :] = block[...]


def local_kernel(hbm_decay, pos, rates, places, terms, decay, wide, sems):
    [copy] = fetch([hbm_decay], [decay], sems)
    places[...] = jnp.zeros_like(places)
    wide[...] = jnp.zeros_like(wide)
    copy.wait()
    for k in range(rates.shape[0]):
        rates[k : k + 1, :] = jnp.full((1, rates.shape[1]), decay[k], F32)
    for t in range(2):
        places[t, 0:3, :] = pos[:, t * TILE : (t + 1) * TILE]
        at = [places[t][c : c + 1, :] for c in range(3)]
        row = iota((8, TILE), 0)
        factors = jnp.where(row == 0, at[0] * at[0] + at[1] * at[1] + at[2] * at[2], 0.0)
        factors = jnp.where(row == 1, 1.0, factors)
        for c in range(3):
            factors = jnp.where(row == 2 + c, at[c], factors)
        high, mid, low = split3(factors)
        for n, part in enumerate((high, mid, low, high, mid, high, mid, low)):
            wide[8 * n : 8 * n + 8, :] = part
        terms[t] = jnp.transpose(wide[...]).astype(BF16)[:, 0:DEPTH]


def plan_kernel(count, lists, rates, plan, reals):
    rep = lax.axis_index("rep")
    lanes = lists.shape[1]
    table = lists[0:8, :] + lists[8:16, :] + lists[16:24, :] + lists[24:32, :]
    home, other = table[0:1, :], table[1:2, :]
    valid = jnp.where(iota((1, lanes), 1) < 4 * count, 1, 0)
    ahead = ones_where(iota((lanes, lanes), 0) < iota((lanes, lanes), 1))

    def before(first, second):
        both = jnp.where(iota((16, lanes), 0) < 8, first, second)
        found = dot(both.astype(F32).astype(BF16), ahead).astype(I32)
        return found[0:1, :], found[8:9, :]

    def total(x):
        return jnp.sum(x.astype(F32), axis=1, keepdims=True).astype(I32)

    local = jnp.where(other < 2, valid, 0)
    start = jnp.zeros((1, 1), I32)
    quota = jnp.zeros((1, 1), I32)
    for q in range(4):
        room = jnp.maximum(count - total(jnp.where(other == 2 + q, valid, 0)), 0)
        start = start + jnp.where(q < rep, room, 0)
        quota = quota + jnp.where(q == rep, room, 0)
    turn, _ = before(local, local)
    taken = jnp.where(turn >= start, local, 0) * jnp.where(turn < start + quota, 1, 0)
    mine = taken + jnp.where(other == 2 + rep, valid, 0)
    first = jnp.where(home == 0, mine, 0)
    second = mine - first
    place_first, place_second = before(first, second)
    quads_first = (total(first) + (QUAD - 1)) // QUAD
    quads_second = (total(second) + (QUAD - 1)) // QUAD
    place = jnp.where(first > 0, place_first, place_second + quads_first * QUAD)
    place = jnp.where(mine > 0, place, -1)
    put = ones_where(iota((lanes, lanes), 0) == place)
    row = iota((8, lanes), 0)
    fields = jnp.where(row == 1, jnp.minimum(table, 2), table)
    fields = jnp.where(row == 6, 1, fields).astype(F32)
    rate = jnp.zeros((1, lanes), F32)
    for k in range(rates.shape[0]):
        rate = jnp.where(table[2:3, :] == k, rates[k : k + 1, :], rate)
    parts = split3(rate)
    rate = jnp.zeros((8, lanes), F32)
    for n in range(3):
        rate = jnp.where(row == n, parts[n], rate)
    fields = jnp.concatenate([fields, rate], axis=0).astype(BF16)
    listed = dot(fields, put, NT)
    counts = listed[0:8, :].astype(I32)
    plan[...] = jnp.where(row == 7, quads_first + quads_second, counts)
    rate = listed[8:9, :] + listed[9:10, :] + listed[10:11, :]
    empty = 1.0 - listed[6:7, :]
    reals[...] = jnp.where(row == 0, rate + empty, jnp.where(row == 7, empty * FAR, listed[0:8, :] * EDGE))


def halo_places(halo):
    side = halo[TILE : TILE + SIDE, :].astype(F32)
    return side[0:8, 0:TILE] + side[8:16, 0:TILE] + side[0:8, TILE : 2 * TILE]


def pair_fields(plan, reals, p):
    return plan[1, p], plan[2, p], reals[0, p], [reals[3 + c, p] for c in range(3)], reals[7, p]


def exponent(terms, places, slot, rate, shift, away):
    at = [places[slot][c : c + 1, :] + shift[c] for c in range(3)]
    at[0] = at[0] + away
    row = iota((8, TILE), 0)
    square = at[0] * at[0] + at[1] * at[1] + at[2] * at[2]
    factors = jnp.where(row == 0, -rate, jnp.where(row == 1, -rate * square, 0.0))
    for c in range(3):
        factors = jnp.where(row == 2 + c, at[c] * (2.0 * rate), factors)
    high, mid, low = split3(factors)
    across = jnp.concatenate([high, high, high, mid, mid, low, low, mid], axis=0).astype(BF16)
    return dot(terms, across)


def halo_kernel(halo, home_places, radial, feat, mapped, places):
    atoms = feat.shape[0]
    places[0:2] = home_places[...]
    places[2] = halo_places(halo)
    for k in range(radial.shape[0]):
        mapped[k, 0:atoms, :] = dot(feat[...], radial[k]).astype(BF16)
        mapped[k, atoms : atoms + TILE, :] = dot(halo[0:TILE, :], radial[k]).astype(BF16)


def forward_kernel(hbm_plan, hbm_reals, terms, mapped, places, partial, plan, reals, message, held, sems):
    copies = fetch((hbm_plan, hbm_reals), (plan, reals), sems)
    atoms = 2 * TILE
    message[...] = jnp.zeros_like(message)
    for copy in copies:
        copy.wait()

    held[...] = jnp.zeros_like(held)
    steps = plan[7, 0]

    def step(q, carry):
        now, ago = jnp.minimum(q, steps - 1) * QUAD, jnp.maximum(q - 1, 0) * QUAD
        home = plan[0, now]
        fields = [pair_fields(plan, reals, now + u) for u in range(QUAD)]
        powers = [exponent(terms[home], places, f[0], *f[2:]) for f in fields]
        across = [mapped[plan[2, ago + u], tile_of(plan[1, ago + u]), :] for u in range(QUAD)]
        message[plan[0, ago]] += dot(held[...], jnp.concatenate(across, axis=0))
        for u in range(QUAD):
            held[:, u * TILE : (u + 1) * TILE] = jnp.exp(powers[u]).astype(BF16)
        return carry

    lax.fori_loop(0, jnp.where(steps > 0, steps + 1, 0), step, 0)
    for t in range(2):
        low = message[t].astype(BF16)
        for q in range(4):
            partial[q * atoms + t * TILE : q * atoms + (t + 1) * TILE, :] = low


def tile_of(slot):
    return pl.ds(pl.multiple_of(slot * TILE, TILE), TILE)


def marks(*which):
    row = iota((SIDE, TILE), 0)
    found = jnp.zeros((SIDE, TILE), F32)
    for r in which:
        found = jnp.where(row == r, 1.0, found)
    return found


def tile_sums(found, block, side):
    found = found[0:SIDE] + found[SIDE : 2 * SIDE]
    at = [block[c : c + 1, :] for c in range(3)]
    zeroth = found[0:1, :]
    once = [found[1 + c : 2 + c, :] for c in range(3)]
    side[...] = jnp.zeros_like(side)
    for c in range(3):
        side[c : c + 1, :] = once[c] - at[c] * zeroth
    for n, (a, b) in enumerate(COMPONENT_PAIRS):
        at_row = 4 + n if n < 3 else 5 + n
        twice = found[at_row : at_row + 1, :]
        side[8 + n : 9 + n, :] = -0.5 * (twice - at[b] * once[a] - at[a] * once[b] + at[a] * at[b] * zeroth)


def atom_kernel(partial, mixing, readout, adjoint, flipped, mixing_part):
    rep = lax.axis_index("rep")
    channels = mixing.shape[0]
    atoms = 2 * TILE
    message = partial[0:atoms, :].astype(F32)
    for q in range(1, 4):
        message = message + partial[q * atoms : (q + 1) * atoms, :].astype(F32)
    packed = message.astype(BF16)
    mixed = dot(packed, mixing[...])
    gate = jax.nn.sigmoid(mixed)
    slope = (readout[...] * gate * (1.0 + mixed * (1.0 - gate))).astype(BF16)
    adjoint[...] = dot(slope, mixing[...], NT).astype(BF16).reshape(2, TILE, channels)
    for t in range(2):
        flipped[t] = dot(mixing[...], slope[t * TILE : (t + 1) * TILE, :], NT).astype(BF16)
    half = channels // 2
    share = channels // 4
    gradient = None
    for odd in range(2):
        take_rows = ones_where(iota((half, channels), 1) == 2 * iota((half, channels), 0) + odd)
        lane = iota((channels, TILE), 1) - odd * share
        inside = jnp.where(lane >= 0, 1, 0) * jnp.where(lane < share, 1, 0)
        take_cols = ones_where(jnp.where(inside > 0, lane + rep * share, -1) == iota((channels, TILE), 0))
        left = dot(take_rows, packed, NT).astype(BF16)
        right = dot(slope, take_cols).astype(BF16)
        part = dot(left, right)
        gradient = part if gradient is None else gradient + part
    mixing_part[...] = gradient


def backward_kernel(
    hbm_plan, hbm_reals, adjoint, flipped, places, terms, radial, mapped,
    back, home_grads, home_sums,
    plan, reals, spread, grads, bases, sums, side, held, weights, sems,
):
    copies = fetch((hbm_plan, hbm_reals), (plan, reals), sems)
    kinds = radial.shape[0]
    for t in range(2):
        for k in range(kinds):
            spread[t * kinds + k] = dot(radial[k], flipped[t]).astype(BF16)

    left_marks = (marks(1, 4, 8, 9), marks(2, 5, 10), marks(3, 6))
    right_marks = (marks(4), marks(5, 8), marks(6, 9, 10))
    left_one, right_one = marks(0), marks(0, 1, 2, 3)
    for t in range(SLOTS):
        block = places[t]
        left, right = left_one, right_one
        for c in range(3):
            left = left + left_marks[c] * block[c : c + 1, :]
            right = right + right_marks[c] * block[c : c + 1, :]
        bases[t, 0:SIDE, :] = left
        bases[t, SIDE : 2 * SIDE, :] = right
    sums[...] = jnp.zeros_like(sums)
    grads[...] = jnp.zeros_like(grads)
    for copy in copies:
        copy.wait()

    def monomials(t, left_shift, right_shift):
        base = bases[t]
        high, low = split((base[0:SIDE] + left_shift) * (base[SIDE : 2 * SIDE] + right_shift))
        both = jnp.concatenate([high, low], axis=0).astype(BF16)
        return jnp.concatenate([both, both], axis=1)

    held[...] = jnp.zeros_like(held)
    weights[...] = jnp.zeros_like(weights)
    steps = plan[7, 0]

    def step(q, carry):
        now, ago = jnp.minimum(q, steps - 1) * QUAD, jnp.maximum(q - 1, 0) * QUAD
        home, home_ago = plan[0, now], plan[0, ago]
        home_sum = None
        for u in range(QUAD):
            slot, kind, rate, shift, away = pair_fields(plan, reals, now + u)
            power = exponent(terms[home], places, slot, rate, shift, away)
            pull = dot(adjoint[home], mapped[kind, tile_of(slot), :], NT)

            slot, kind, _, shift, _ = pair_fields(plan, reals, ago + u)
            left_shift = sum(left_marks[c] * shift[c] for c in range(3))
            right_shift = sum(right_marks[c] * shift[c] for c in range(3))
            far = monomials(slot, left_shift, right_shift)
            near = monomials(home_ago, -left_shift, -right_shift)
            high, low = weights[u, 0], weights[u, 1]
            part = dot(far, jnp.concatenate([high, low], axis=1), NT)
            home_sum = part if home_sum is None else home_sum + part
            sums[slot] += dot(near, jnp.concatenate([high, low], axis=0))
            grads[slot] += dot(spread[home_ago * kinds + kind], held[u])

            kernel = jnp.exp(power)
            held[u] = kernel.astype(BF16)
            weight = (kernel * (-2.0 * rate)) * pull
            high = weight.astype(BF16)
            weights[u, 0] = high
            weights[u, 1] = (weight - high.astype(F32)).astype(BF16)
        sums[home_ago] += home_sum
        return carry

    lax.fori_loop(0, jnp.where(steps > 0, steps + 1, 0), step, 0)
    back[0:TILE, :] = jnp.transpose(grads[2]).astype(BF16)
    tile_sums(sums[2], places[2], side)
    high, low = split(side[...])
    back[TILE : TILE + SIDE, 0:TILE] = high.astype(BF16)
    back[TILE : TILE + SIDE, TILE : 2 * TILE] = low.astype(BF16)
    home_grads[...] = grads[0:2]
    home_sums[...] = sums[0:2]


def own_kernel(home_grads, home_sums, places, own_grad, own_side, side):
    for t in range(2):
        own_grad[t * TILE : (t + 1) * TILE, :] = jnp.transpose(home_grads[t])
        tile_sums(home_sums[t], places[t], side)
        own_side[:, t * TILE : (t + 1) * TILE] = side[...]


def return_kernel(rows, got, own_grad, own_side, payload):
    rep = lax.axis_index("rep")
    atoms = own_grad.shape[0]
    pick = ones_where(iota((atoms, TILE), 0) == rows[pl.ds(rep, 1), :])
    grad = (own_grad[...] + dot(pick, got[0:TILE, :])).astype(BF16)
    came = got[TILE : TILE + SIDE, :]
    side = own_side[...] + dot(came[:, 0:TILE], pick, NT) + dot(came[:, TILE : 2 * TILE], pick, NT)
    high, low = split(side)
    both = jnp.concatenate([high, low], axis=0).astype(BF16)
    height = atoms + 2 * SIDE
    for q in range(4):
        payload[q * height : q * height + atoms, :] = grad
        payload[q * height + atoms : (q + 1) * height, :] = both


def final_kernel(payload, grad, forces, virials):
    atoms = grad.shape[0]
    height = atoms + 2 * SIDE
    total = None
    side = None
    for q in range(4):
        part = payload[q * height : q * height + atoms, :].astype(F32)
        total = part if total is None else total + part
        both = payload[q * height + atoms : (q + 1) * height, :].astype(F32)
        part = both[0:SIDE] + both[SIDE : 2 * SIDE]
        side = part if side is None else side + part
    grad[...] = total.astype(BF16)
    forces[...] = side[0:3]
    virials[...] = side[8:14]


def mixing_kernel(mixing_parts, grad_mixing):
    found = jnp.sum(mixing_parts[...], axis=0, keepdims=True)
    share = grad_mixing.shape[1]
    grad_mixing[0:1, :] = found[:, 0:share]
    grad_mixing[1:2, :] = found[:, share : 2 * share]


def call(kernel, outs, ins, scratch=(), hbm=0, sems=0, away=(), flops=0, moved=1 << 20, limit=32 << 20):
    vmem = pl.BlockSpec(memory_space=pltpu.VMEM)
    stay = pl.BlockSpec(memory_space=pl.ANY)
    return pl.pallas_call(
        kernel,
        out_shape=[jax.ShapeDtypeStruct(shape, dtype) for shape, dtype in outs],
        in_specs=[stay if n < hbm or n in away else vmem for n in range(len(ins))],
        out_specs=[vmem] * len(outs),
        scratch_shapes=list(scratch) + ([pltpu.SemaphoreType.DMA((sems,))] if sems else []),
        compiler_params=pltpu.CompilerParams(vmem_limit_bytes=limit),
        cost_estimate=pl.CostEstimate(flops=flops, bytes_accessed=moved, transcendentals=0),
    )(*ins)


def on_device(
    features, positions, radial, mixing, readout, decay,
    send_rows, pair_home, pair_other, pair_kind, pair_image,
):
    atoms, channels = features.shape
    kinds = radial.shape[0]
    count = pair_home.shape[0]
    doms, reps = lax.axis_size("dom"), lax.axis_size("rep")
    lanes = 2 * TILE
    height = atoms + 2 * SIDE
    assert reps == len(OFFSETS) and atoms == 2 * TILE and 4 * count <= lanes - 4 * QUAD
    assert channels == 2 * doms

    def hop(array, sign):
        ways = [
            (d * reps + r, (d + sign * OFFSETS[r]) % doms * reps + r)
            for d in range(doms)
            for r in range(reps)
        ]
        return lax.ppermute(array, ("dom", "rep"), ways)

    def swap(array, axis):
        return lax.all_to_all(array, axis, 0, 0, tiled=True)

    vmem, smem = pltpu.VMEM, pltpu.SMEM
    sent = [send_rows, *(x.reshape(1, count) for x in (pair_home, pair_other, pair_kind))]
    sent += [pair_image, positions, features]
    send, lists = call(
        pack_kernel,
        [((TILE + SIDE, channels), BF16), ((32, lanes), I32)],
        sent,
        [vmem(x.shape, x.dtype) for x in sent[:5]]
        + [vmem((8, atoms), F32), vmem(features.shape, BF16), vmem((8, lanes), I32)],
        hbm=len(sent),
        sems=len(sent),
        flops=1 << 30,
        limit=63 << 20,
    )
    halo = hop(send, 1)
    lists = swap(lists, "rep")
    rates, home_places, terms = call(
        local_kernel,
        [((kinds, lanes), F32), ((2, 8, TILE), F32), ((2, TILE, DEPTH), BF16)],
        [decay, positions],
        [smem(decay.shape, F32), vmem((TILE, TILE), F32)],
        hbm=1,
        sems=1,
        flops=1 << 32,
    )
    plan, reals = call(
        functools.partial(plan_kernel, count),
        [((8, lanes), I32), ((8, lanes), F32)],
        [lists, rates],
        flops=1 << 20,
    )
    tables = [smem((8, lanes), I32), smem((8, lanes), F32)]
    mapped, places = call(
        halo_kernel,
        [((kinds, SLOTS * TILE, channels), BF16), ((SLOTS, 8, TILE), F32)],
        [halo, home_places, radial, features],
        flops=1 << 30,
    )
    [partial] = call(
        forward_kernel,
        [((reps * atoms, channels), BF16)],
        [plan, reals, terms, mapped, places],
        tables + [vmem((2, TILE, channels), F32), vmem((TILE, QUAD * TILE), BF16)],
        hbm=2,
        sems=2,
        flops=1 << 31,
    )
    partial = swap(partial, "rep")
    adjoint, flipped, mixing_part = call(
        atom_kernel,
        [((2, TILE, channels), BF16), ((2, channels, TILE), BF16), ((channels // 2, TILE), F32)],
        [partial, mixing, readout.reshape(1, channels)],
        flops=1 << 28,
    )
    mixing_parts = swap(mixing_part, "dom")
    back, home_grads, home_sums = call(
        backward_kernel,
        [((TILE + SIDE, channels), BF16), ((2, channels, TILE), F32), ((2, 2 * SIDE, TILE), F32)],
        [plan, reals, adjoint, flipped, places, terms, radial, mapped],
        tables
        + [
            vmem((2 * kinds, channels, TILE), BF16),
            vmem((SLOTS, channels, TILE), F32),
            vmem((SLOTS, 2 * SIDE, TILE), F32),
            vmem((SLOTS, 2 * SIDE, TILE), F32),
            vmem((SIDE, TILE), F32),
            vmem((QUAD, TILE, TILE), BF16),
            vmem((QUAD, 2, TILE, TILE), BF16),
        ],
        hbm=2,
        sems=2,
        flops=1 << 33,
    )
    got = hop(back, -1)
    own_grad, own_side = call(
        own_kernel,
        [((atoms, channels), F32), ((SIDE, atoms), F32)],
        [home_grads, home_sums, places],
        [vmem((SIDE, TILE), F32)],
        flops=1 << 30,
    )
    [payload] = call(
        return_kernel,
        [((reps * height, channels), BF16)],
        [send_rows, got, own_grad, own_side],
        flops=1 << 24,
    )
    payload = swap(payload, "rep")
    [grad_mixing] = call(mixing_kernel, [((2, channels // reps), F32)], [mixing_parts])
    grad, forces, virials = call(
        final_kernel,
        [((atoms, channels), BF16), ((3, atoms), F32), ((6, atoms), F32)],
        [payload],
    )
    return grad, forces, virials, grad_mixing


def solution(mesh):
    in_specs = (
        P("dom", None),
        P(None, "dom"),
        P(),
        P(),
        P(),
        P(),
        P(None, "dom"),
        P(("dom", "rep")),
        P(("dom", "rep")),
        P(("dom", "rep")),
        P(None, ("dom", "rep")),
    )
    out_specs = (P("dom", None), P(None, "dom"), P(None, "dom"), P("dom", "rep"))
    return jax.shard_map(
        on_device, mesh=mesh, in_specs=in_specs, out_specs=out_specs, check_vma=False
    )
```

```python
import functools

import jax
import jax.numpy as jnp
from jax import lax
from jax.experimental import pallas as pl
from jax.experimental.pallas import tpu as pltpu
from jax.sharding import PartitionSpec as P

TILE = 128
SLOTS = 3
QUAD = 8
SIDE = 16
OFFSETS = (1, -1, 2, -2)
EDGE = 2.0
FAR = 1.0e4
DEPTH = 64
F32, BF16, I32 = jnp.float32, jnp.bfloat16, jnp.int32
COMPONENT_PAIRS = ((0, 0), (1, 1), (2, 2), (0, 1), (0, 2), (1, 2))

NN = (((1,), (0,)), ((), ()))
NT = (((1,), (1,)), ((), ()))
TN = (((0,), (0,)), ((), ()))


def dot(a, b, dims=NN):
    return lax.dot_general(a, b, dims, preferred_element_type=F32)


def iota(shape, dim):
    return lax.broadcasted_iota(I32, shape, dim)


def ones_where(mask, dtype=BF16):
    return jnp.where(mask, 1.0, 0.0).astype(dtype)


def split(x):
    high = x.astype(BF16).astype(F32)
    return high, (x - high).astype(BF16).astype(F32)


def split3(x):
    high, mid = split(x)
    return high, mid, x - high - mid


def fetch(sources, targets, sems):
    copies = [pltpu.make_async_copy(a, b, sems.at[n]) for n, (a, b) in enumerate(zip(sources, targets))]
    for copy in copies:
        copy.start()
    return copies


def pack_kernel(
    hbm_rows, hbm_home, hbm_other, hbm_kind, hbm_image, hbm_pos, hbm_feat,
    send, lists,
    rows, home, other, kind, image, pos, feat, block, sems,
):
    copies = fetch(
        (hbm_rows, hbm_home, hbm_other, hbm_kind, hbm_image, hbm_pos, hbm_feat),
        (rows, home, other, kind, image, pos.at[0:3, :], feat),
        sems,
    )
    rep = lax.axis_index("rep")
    atoms = feat.shape[0]
    count = home.shape[1]
    pos[3:8, :] = jnp.zeros((5, atoms), F32)
    block[...] = jnp.zeros_like(block)
    for copy in copies:
        copy.wait()
    pick = ones_where(iota((atoms, TILE), 0) == rows[pl.ds(rep, 1), :])
    send[0:TILE, :] = dot(pick, feat[...], TN).astype(BF16)
    parts = jnp.concatenate([*split3(pos[...]), jnp.zeros_like(pos)], axis=0).astype(BF16)
    moved = dot(parts, pick).astype(BF16)
    send[TILE : TILE + SIDE, 0:TILE] = moved[0:SIDE]
    send[TILE : TILE + SIDE, TILE : 2 * TILE] = moved[SIDE : 2 * SIDE]
    for q in range(4):

        @pl.when(rep == q)
        def _(q=q):
            span = slice(q * count, (q + 1) * count)
            block[0:1, span] = home[...]
            block[1:2, span] = other[...]
            block[2:3, span] = kind[...]
            block[3:6, span] = image[...]

    for q in range(4):
        lists[8 * q : 8 * q + 8, :] = block[...]


def local_kernel(hbm_decay, pos, rates, places, terms, decay, wide, sems):
    [copy] = fetch([hbm_decay], [decay], sems)
    places[...] = jnp.zeros_like(places)
    wide[...] = jnp.zeros_like(wide)
    copy.wait()
    for k in range(rates.shape[0]):
        rates[k : k + 1, :] = jnp.full((1, rates.shape[1]), decay[k], F32)
    for t in range(2):
        places[t, 0:3, :] = pos[:, t * TILE : (t + 1) * TILE]
        terms[t] = tile_terms(places[t], wide)


def plan_kernel(count, lists, rates, plan, reals):
    rep = lax.axis_index("rep")
    lanes = lists.shape[1]
    table = lists[0:8, :] + lists[8:16, :] + lists[16:24, :] + lists[24:32, :]
    home, other = table[0:1, :], table[1:2, :]
    valid = jnp.where(iota((1, lanes), 1) < 4 * count, 1, 0)
    ahead = ones_where(iota((lanes, lanes), 0) < iota((lanes, lanes), 1))

    def before(first, second):
        both = jnp.where(iota((16, lanes), 0) < 8, first, second)
        found = dot(both.astype(F32).astype(BF16), ahead).astype(I32)
        return found[0:1, :], found[8:9, :]

    def total(x):
        return jnp.sum(x.astype(F32), axis=1, keepdims=True).astype(I32)

    local = jnp.where(other < 2, valid, 0)
    start = jnp.zeros((1, 1), I32)
    quota = jnp.zeros((1, 1), I32)
    for q in range(4):
        room = jnp.maximum(count - total(jnp.where(other == 2 + q, valid, 0)), 0)
        start = start + jnp.where(q < rep, room, 0)
        quota = quota + jnp.where(q == rep, room, 0)
    turn, _ = before(local, local)
    taken = jnp.where(turn >= start, local, 0) * jnp.where(turn < start + quota, 1, 0)
    mine = taken + jnp.where(other == 2 + rep, valid, 0)
    first = jnp.where(home == 0, mine, 0)
    second = mine - first
    place_first, place_second = before(first, second)
    quads_first = (total(first) + (QUAD - 1)) // QUAD
    quads_second = (total(second) + (QUAD - 1)) // QUAD
    place = jnp.where(first > 0, place_first, place_second + quads_first * QUAD)
    place = jnp.where(mine > 0, place, -1)
    put = ones_where(iota((lanes, lanes), 0) == place)
    row = iota((8, lanes), 0)
    fields = jnp.where(row == 1, jnp.minimum(table, 2), table)
    fields = jnp.where(row == 6, 1, fields).astype(F32)
    rate = jnp.zeros((1, lanes), F32)
    for k in range(rates.shape[0]):
        rate = jnp.where(table[2:3, :] == k, rates[k : k + 1, :], rate)
    parts = split3(rate)
    rate = jnp.zeros((8, lanes), F32)
    for n in range(3):
        rate = jnp.where(row == n, parts[n], rate)
    fields = jnp.concatenate([fields, rate], axis=0).astype(BF16)
    listed = dot(fields, put, NT)
    counts = listed[0:8, :].astype(I32)
    plan[...] = jnp.where(row == 7, quads_first + quads_second, counts)
    rate = listed[8:9, :] + listed[9:10, :] + listed[10:11, :]
    empty = 1.0 - listed[6:7, :]
    reals[...] = jnp.where(row == 0, rate + empty, jnp.where(row == 7, empty * FAR, listed[0:8, :] * EDGE))


def halo_places(halo):
    side = halo[TILE : TILE + SIDE, :].astype(F32)
    return side[0:8, 0:TILE] + side[8:16, 0:TILE] + side[0:8, TILE : 2 * TILE]


def pair_fields(plan, reals, p):
    return plan[1, p], plan[2, p], reals[0, p], [reals[3 + c, p] for c in range(3)], reals[7, p]


def exponent_factors(block, rate, shift, away):
    at = [block[c : c + 1, :] + shift[c] for c in range(3)]
    at[0] = at[0] + away
    row = iota((8, TILE), 0)
    square = at[0] * at[0] + at[1] * at[1] + at[2] * at[2]
    factors = jnp.where(row == 0, -rate, jnp.where(row == 1, -rate * square, 0.0))
    for c in range(3):
        factors = jnp.where(row == 2 + c, at[c] * (2.0 * rate), factors)
    high, mid, low = split3(factors)
    return jnp.concatenate([high, high, high, mid, mid, low, low, mid], axis=0).astype(BF16)


def tile_terms(block, wide):
    at = [block[c : c + 1, :] for c in range(3)]
    row = iota((8, TILE), 0)
    factors = jnp.where(row == 0, at[0] * at[0] + at[1] * at[1] + at[2] * at[2], 0.0)
    factors = jnp.where(row == 1, 1.0, factors)
    for c in range(3):
        factors = jnp.where(row == 2 + c, at[c], factors)
    high, mid, low = split3(factors)
    for n, part in enumerate((high, mid, low, high, mid, high, mid, low)):
        wide[8 * n : 8 * n + 8, :] = part
    return jnp.transpose(wide[...]).astype(BF16)[:, 0:DEPTH]


def forward_kernel(
    hbm_plan, hbm_reals, halo, home_places, home_terms, radial, feat,
    mapped, places, terms, partial,
    plan, reals, wide, message, held, sems,
):
    copies = fetch((hbm_plan, hbm_reals), (plan, reals), sems)
    atoms = feat.shape[0]
    places[0:2] = home_places[...]
    places[2] = halo_places(halo)
    terms[0:2] = home_terms[...]
    wide[...] = jnp.zeros_like(wide)
    terms[2] = tile_terms(places[2], wide)
    for k in range(radial.shape[0]):
        mapped[k, 0:atoms, :] = dot(feat[...], radial[k]).astype(BF16)
        mapped[k, atoms : atoms + TILE, :] = dot(halo[0:TILE, :], radial[k]).astype(BF16)
    message[...] = jnp.zeros_like(message)
    for copy in copies:
        copy.wait()

    steps = plan[7, 0]

    def powers(q):
        terms_home = terms[plan[0, q * QUAD]]
        fields = [pair_fields(plan, reals, q * QUAD + u) for u in range(QUAD)]
        return [dot(terms_home, exponent_factors(places[f[0]], *f[2:])) for f in fields]

    def hold(found):
        for u in range(QUAD):
            held[:, u * TILE : (u + 1) * TILE] = jnp.exp(found[u]).astype(BF16)

    def products(q):
        first = q * QUAD
        across = [mapped[plan[2, first + u], tile_of(plan[1, first + u]), :] for u in range(QUAD)]
        message[plan[0, first]] += dot(held[...], jnp.concatenate(across, axis=0))

    def step(q, carry):
        found = powers(q)
        products(q - 1)
        hold(found)
        return carry

    @pl.when(steps > 0)
    def _():
        hold(powers(0))
        lax.fori_loop(1, steps, step, 0)
        products(steps - 1)

    for t in range(2):
        low = message[t].astype(BF16)
        for q in range(4):
            partial[q * atoms + t * TILE : q * atoms + (t + 1) * TILE, :] = low


def tile_of(slot):
    return pl.ds(pl.multiple_of(slot * TILE, TILE), TILE)


def marks(*which):
    row = iota((SIDE, TILE), 0)
    found = jnp.zeros((SIDE, TILE), F32)
    for r in which:
        found = jnp.where(row == r, 1.0, found)
    return found


def tile_sums(found, block, side):
    found = found[0:SIDE] + found[SIDE : 2 * SIDE]
    at = [block[c : c + 1, :] for c in range(3)]
    zeroth = found[0:1, :]
    once = [found[1 + c : 2 + c, :] for c in range(3)]
    side[...] = jnp.zeros_like(side)
    for c in range(3):
        side[c : c + 1, :] = once[c] - at[c] * zeroth
    for n, (a, b) in enumerate(COMPONENT_PAIRS):
        at_row = 4 + n if n < 3 else 5 + n
        twice = found[at_row : at_row + 1, :]
        side[8 + n : 9 + n, :] = -0.5 * (twice - at[b] * once[a] - at[a] * once[b] + at[a] * at[b] * zeroth)


def atom_kernel(partial, mixing, readout, adjoint, flipped, mixing_part):
    rep = lax.axis_index("rep")
    channels = mixing.shape[0]
    atoms = 2 * TILE
    message = partial[0:atoms, :].astype(F32)
    for q in range(1, 4):
        message = message + partial[q * atoms : (q + 1) * atoms, :].astype(F32)
    packed = message.astype(BF16)
    mixed = dot(packed, mixing[...])
    gate = jax.nn.sigmoid(mixed)
    slope = (readout[...] * gate * (1.0 + mixed * (1.0 - gate))).astype(BF16)
    adjoint[...] = dot(slope, mixing[...], NT).astype(BF16)
    for t in range(2):
        flipped[t] = dot(mixing[...], slope[t * TILE : (t + 1) * TILE, :], NT).astype(BF16)
    half = channels // 2
    share = channels // 4
    gradient = None
    for odd in range(2):
        take_rows = ones_where(iota((half, channels), 1) == 2 * iota((half, channels), 0) + odd)
        lane = iota((channels, TILE), 1) - odd * share
        inside = jnp.where(lane >= 0, 1, 0) * jnp.where(lane < share, 1, 0)
        take_cols = ones_where(jnp.where(inside > 0, lane + rep * share, -1) == iota((channels, TILE), 0))
        left = dot(take_rows, packed, NT).astype(BF16)
        right = dot(slope, take_cols).astype(BF16)
        part = dot(left, right)
        gradient = part if gradient is None else gradient + part
    mixing_part[...] = gradient


def backward_kernel(
    hbm_plan, hbm_reals, adjoint, flipped, places, terms, radial, mapped,
    back, home_grads, home_sums,
    plan, reals, spread, grads, bases, sums, side, held, weights, sems,
):
    copies = fetch((hbm_plan, hbm_reals), (plan, reals), sems)
    kinds = radial.shape[0]
    for k in range(kinds):
        spread[k] = dot(adjoint[...], radial[k], NT).astype(BF16)

    left_marks = (marks(1, 4, 8, 9), marks(2, 5, 10), marks(3, 6))
    right_marks = (marks(4), marks(5, 8), marks(6, 9, 10))
    left_one, right_one = marks(0), marks(0, 1, 2, 3)
    for t in range(SLOTS):
        block = places[t]
        left, right = left_one, right_one
        for c in range(3):
            left = left + left_marks[c] * block[c : c + 1, :]
            right = right + right_marks[c] * block[c : c + 1, :]
        bases[t, 0:SIDE, :] = left
        bases[t, SIDE : 2 * SIDE, :] = right
    sums[...] = jnp.zeros_like(sums)
    grads[...] = jnp.zeros_like(grads)
    for copy in copies:
        copy.wait()

    def monomials(t, left_shift, right_shift):
        base = bases[t]
        high, low = split((base[0:SIDE] + left_shift) * (base[SIDE : 2 * SIDE] + right_shift))
        both = jnp.concatenate([high, low], axis=0).astype(BF16)
        return jnp.concatenate([both, both], axis=1)

    steps = plan[7, 0]

    def begin(q):
        first = q * QUAD
        home = plan[0, first]
        fields = [pair_fields(plan, reals, first + u) for u in range(QUAD)]
        tiles = [mapped[kind, tile_of(slot), :] for slot, kind, *_ in fields]
        pulls = dot(jnp.concatenate(tiles, axis=0), flipped[home])
        block = places[home]
        powers = [
            dot(terms[slot], exponent_factors(block, rate, [-x for x in shift], away))
            for slot, _, rate, shift, away in fields
        ]
        return [(powers[u], pulls[u * TILE : (u + 1) * TILE], fields[u][2]) for u in range(QUAD)]

    def hold(u, power, pull, rate):
        kernel = jnp.exp(power)
        held[u] = kernel.astype(BF16)
        weight = (kernel * (-2.0 * rate)) * pull
        high = weight.astype(BF16)
        weights[u, 0] = high
        weights[u, 1] = (weight - high.astype(F32)).astype(BF16)

    def finish(q, u):
        home = plan[0, q * QUAD]
        slot, kind, _, shift, _ = pair_fields(plan, reals, q * QUAD + u)
        left_shift = sum(left_marks[c] * shift[c] for c in range(3))
        right_shift = sum(right_marks[c] * shift[c] for c in range(3))
        far = monomials(slot, left_shift, right_shift)
        near = monomials(home, -left_shift, -right_shift)
        high, low = weights[u, 0], weights[u, 1]
        sums[slot] += dot(near, jnp.concatenate([high, low], axis=1), NT)
        grads[slot] += dot(held[u], spread[kind, tile_of(home), :])
        return dot(far, jnp.concatenate([high, low], axis=0))

    def step(q, carry):
        found = begin(q)
        parts = []
        for u in range(QUAD):
            parts.append(finish(q - 1, u))
            hold(u, *found[u])
        sums[plan[0, (q - 1) * QUAD]] += sum(parts[1:], parts[0])
        return carry

    @pl.when(steps > 0)
    def _():
        for u, found in enumerate(begin(0)):
            hold(u, *found)
        lax.fori_loop(1, steps, step, 0)
        parts = [finish(steps - 1, u) for u in range(QUAD)]
        sums[plan[0, (steps - 1) * QUAD]] += sum(parts[1:], parts[0])

    back[0:TILE, :] = grads[2].astype(BF16)
    tile_sums(sums[2], places[2], side)
    high, low = split(side[...])
    back[TILE : TILE + SIDE, 0:TILE] = high.astype(BF16)
    back[TILE : TILE + SIDE, TILE : 2 * TILE] = low.astype(BF16)
    home_grads[...] = grads[0:2].reshape(home_grads.shape)
    home_sums[...] = sums[0:2]


def own_kernel(home_sums, places, own_side, side):
    for t in range(2):
        tile_sums(home_sums[t], places[t], side)
        own_side[:, t * TILE : (t + 1) * TILE] = side[...]


def return_kernel(rows, got, own_grad, own_side, payload):
    rep = lax.axis_index("rep")
    atoms = own_grad.shape[0]
    pick = ones_where(iota((atoms, TILE), 0) == rows[pl.ds(rep, 1), :])
    grad = (own_grad[...] + dot(pick, got[0:TILE, :])).astype(BF16)
    came = got[TILE : TILE + SIDE, :]
    side = own_side[...] + dot(came[:, 0:TILE], pick, NT) + dot(came[:, TILE : 2 * TILE], pick, NT)
    high, low = split(side)
    both = jnp.concatenate([high, low], axis=0).astype(BF16)
    height = atoms + 2 * SIDE
    for q in range(4):
        payload[q * height : q * height + atoms, :] = grad
        payload[q * height + atoms : (q + 1) * height, :] = both


def final_kernel(payload, mixing_parts, grad, forces, virials, grad_mixing):
    atoms = grad.shape[0]
    height = atoms + 2 * SIDE
    total = None
    side = None
    for q in range(4):
        part = payload[q * height : q * height + atoms, :].astype(F32)
        total = part if total is None else total + part
        both = payload[q * height + atoms : (q + 1) * height, :].astype(F32)
        part = both[0:SIDE] + both[SIDE : 2 * SIDE]
        side = part if side is None else side + part
    grad[...] = total.astype(BF16)
    forces[...] = side[0:3]
    virials[...] = side[8:14]
    found = jnp.sum(mixing_parts[...], axis=0, keepdims=True)
    share = grad_mixing.shape[1]
    grad_mixing[0:1, :] = found[:, 0:share]
    grad_mixing[1:2, :] = found[:, share : 2 * share]


def call(kernel, outs, ins, scratch=(), hbm=0, sems=0, away=(), flops=0, moved=1 << 20, limit=32 << 20):
    vmem = pl.BlockSpec(memory_space=pltpu.VMEM)
    stay = pl.BlockSpec(memory_space=pl.ANY)
    return pl.pallas_call(
        kernel,
        out_shape=[jax.ShapeDtypeStruct(shape, dtype) for shape, dtype in outs],
        in_specs=[stay if n < hbm or n in away else vmem for n in range(len(ins))],
        out_specs=[vmem] * len(outs),
        scratch_shapes=list(scratch) + ([pltpu.SemaphoreType.DMA((sems,))] if sems else []),
        compiler_params=pltpu.CompilerParams(vmem_limit_bytes=limit),
        cost_estimate=pl.CostEstimate(flops=flops, bytes_accessed=moved, transcendentals=0),
    )(*ins)


def on_device(
    features, positions, radial, mixing, readout, decay,
    send_rows, pair_home, pair_other, pair_kind, pair_image,
):
    atoms, channels = features.shape
    kinds = radial.shape[0]
    count = pair_home.shape[0]
    doms, reps = lax.axis_size("dom"), lax.axis_size("rep")
    lanes = 2 * TILE
    height = atoms + 2 * SIDE
    assert reps == len(OFFSETS) and atoms == 2 * TILE and 4 * count <= lanes - 4 * QUAD
    assert channels == 2 * doms

    def hop(array, sign):
        ways = [
            (d * reps + r, (d + sign * OFFSETS[r]) % doms * reps + r)
            for d in range(doms)
            for r in range(reps)
        ]
        return lax.ppermute(array, ("dom", "rep"), ways)

    def swap(array, axis):
        return lax.all_to_all(array, axis, 0, 0, tiled=True)

    vmem, smem = pltpu.VMEM, pltpu.SMEM
    sent = [send_rows, *(x.reshape(1, count) for x in (pair_home, pair_other, pair_kind))]
    sent += [pair_image, positions, features]
    send, lists = call(
        pack_kernel,
        [((TILE + SIDE, channels), BF16), ((32, lanes), I32)],
        sent,
        [vmem(x.shape, x.dtype) for x in sent[:5]]
        + [vmem((8, atoms), F32), vmem(features.shape, BF16), vmem((8, lanes), I32)],
        hbm=len(sent),
        sems=len(sent),
        flops=1 << 30,
        limit=63 << 20,
    )
    halo = hop(send, 1)
    lists = swap(lists, "rep")
    rates, home_places, home_terms = call(
        local_kernel,
        [((kinds, lanes), F32), ((2, 8, TILE), F32), ((2, TILE, DEPTH), BF16)],
        [decay, positions],
        [smem(decay.shape, F32), vmem((TILE, TILE), F32)],
        hbm=1,
        sems=1,
        flops=1 << 32,
    )
    plan, reals = call(
        functools.partial(plan_kernel, count),
        [((8, lanes), I32), ((8, lanes), F32)],
        [lists, rates],
        flops=1 << 20,
    )
    tables = [smem((8, lanes), I32), smem((8, lanes), F32)]
    mapped, places, terms, partial = call(
        forward_kernel,
        [
            ((kinds, SLOTS * TILE, channels), BF16),
            ((SLOTS, 8, TILE), F32),
            ((SLOTS, TILE, DEPTH), BF16),
            ((reps * atoms, channels), BF16),
        ],
        [plan, reals, halo, home_places, home_terms, radial, features],
        tables
        + [vmem((TILE, TILE), F32), vmem((2, TILE, channels), F32), vmem((TILE, QUAD * TILE), BF16)],
        hbm=2,
        sems=2,
        flops=1 << 31,
    )
    partial = swap(partial, "rep")
    adjoint, flipped, mixing_part = call(
        atom_kernel,
        [((atoms, channels), BF16), ((2, channels, TILE), BF16), ((channels // 2, TILE), F32)],
        [partial, mixing, readout.reshape(1, channels)],
        flops=1 << 28,
    )
    mixing_parts = swap(mixing_part, "dom")
    back, own_grad, home_sums = call(
        backward_kernel,
        [((TILE + SIDE, channels), BF16), ((atoms, channels), F32), ((2, 2 * SIDE, TILE), F32)],
        [plan, reals, adjoint, flipped, places, terms, radial, mapped],
        tables
        + [
            vmem((kinds, atoms, channels), BF16),
            vmem((SLOTS, TILE, channels), F32),
            vmem((SLOTS, 2 * SIDE, TILE), F32),
            vmem((SLOTS, 2 * SIDE, TILE), F32),
            vmem((SIDE, TILE), F32),
            vmem((QUAD, TILE, TILE), BF16),
            vmem((QUAD, 2, TILE, TILE), BF16),
        ],
        hbm=2,
        sems=2,
        flops=1 << 33,
    )
    got = hop(back, -1)
    [own_side] = call(
        own_kernel, [((SIDE, atoms), F32)], [home_sums, places], [vmem((SIDE, TILE), F32)], flops=1 << 30
    )
    [payload] = call(
        return_kernel,
        [((reps * height, channels), BF16)],
        [send_rows, got, own_grad, own_side],
        flops=1 << 24,
    )
    payload = swap(payload, "rep")
    return tuple(
        call(
            final_kernel,
            [((atoms, channels), BF16), ((3, atoms), F32), ((6, atoms), F32), ((2, channels // reps), F32)],
            [payload, mixing_parts],
        )
    )


def solution(mesh):
    in_specs = (
        P("dom", None),
        P(None, "dom"),
        P(),
        P(),
        P(),
        P(),
        P(None, "dom"),
        P(("dom", "rep")),
        P(("dom", "rep")),
        P(("dom", "rep")),
        P(None, ("dom", "rep")),
    )
    out_specs = (P("dom", None), P(None, "dom"), P(None, "dom"), P("dom", "rep"))
    return jax.shard_map(
        on_device, mesh=mesh, in_specs=in_specs, out_specs=out_specs, check_vma=False
    )
```

```python
import functools

import jax
import jax.numpy as jnp
from jax import lax
from jax.experimental import pallas as pl
from jax.experimental.pallas import tpu as pltpu
from jax.sharding import PartitionSpec as P

TILE = 128
SLOTS = 3
QUAD = 8
SIDE = 16
OFFSETS = (1, -1, 2, -2)
EDGE = 2.0
FAR = 1.0e4
DEPTH = 64
F32, BF16, I32 = jnp.float32, jnp.bfloat16, jnp.int32
COMPONENT_PAIRS = ((0, 0), (1, 1), (2, 2), (0, 1), (0, 2), (1, 2))

NN = (((1,), (0,)), ((), ()))
NT = (((1,), (1,)), ((), ()))
TN = (((0,), (0,)), ((), ()))


def dot(a, b, dims=NN):
    return lax.dot_general(a, b, dims, preferred_element_type=F32)


def iota(shape, dim):
    return lax.broadcasted_iota(I32, shape, dim)


def ones_where(mask, dtype=BF16):
    return jnp.where(mask, 1.0, 0.0).astype(dtype)


def split(x):
    high = x.astype(BF16).astype(F32)
    return high, (x - high).astype(BF16).astype(F32)


def split3(x):
    high, mid = split(x)
    return high, mid, x - high - mid


def fetch(sources, targets, sems):
    copies = [pltpu.make_async_copy(a, b, sems.at[n]) for n, (a, b) in enumerate(zip(sources, targets))]
    for copy in copies:
        copy.start()
    return copies


def pack_kernel(
    hbm_rows, hbm_home, hbm_other, hbm_kind, hbm_image, hbm_pos, hbm_feat,
    send, lists,
    rows, home, other, kind, image, pos, feat, block, sems,
):
    copies = fetch(
        (hbm_rows, hbm_home, hbm_other, hbm_kind, hbm_image, hbm_pos, hbm_feat),
        (rows, home, other, kind, image, pos.at[0:3, :], feat),
        sems,
    )
    rep = lax.axis_index("rep")
    atoms = feat.shape[0]
    count = home.shape[1]
    pos[3:8, :] = jnp.zeros((5, atoms), F32)
    block[...] = jnp.zeros_like(block)
    for copy in copies:
        copy.wait()
    pick = ones_where(iota((atoms, TILE), 0) == rows[pl.ds(rep, 1), :])
    send[0:TILE, :] = dot(pick, feat[...], TN).astype(BF16)
    parts = jnp.concatenate([*split3(pos[...]), jnp.zeros_like(pos)], axis=0).astype(BF16)
    moved = dot(parts, pick).astype(BF16)
    send[TILE : TILE + SIDE, 0:TILE] = moved[0:SIDE]
    send[TILE : TILE + SIDE, TILE : 2 * TILE] = moved[SIDE : 2 * SIDE]
    for q in range(4):

        @pl.when(rep == q)
        def _(q=q):
            span = slice(q * count, (q + 1) * count)
            block[0:1, span] = home[...]
            block[1:2, span] = other[...]
            block[2:3, span] = kind[...]
            block[3:6, span] = image[...]

    for q in range(4):
        lists[8 * q : 8 * q + 8, :] = block[...]


def local_kernel(
    hbm_decay, hbm_readout, hbm_rows, pos,
    rates, places, terms, readout, rows,
    decay, wide, sems,
):
    copy, *later = fetch([hbm_decay, hbm_readout, hbm_rows], [decay, readout, rows], sems)
    places[...] = jnp.zeros_like(places)
    wide[...] = jnp.zeros_like(wide)
    copy.wait()
    for k in range(rates.shape[0]):
        rates[k : k + 1, :] = jnp.full((1, rates.shape[1]), decay[k], F32)
    for t in range(2):
        places[t, 0:3, :] = pos[:, t * TILE : (t + 1) * TILE]
        terms[t] = tile_terms(places[t], wide)
    for copy in later:
        copy.wait()


def plan_kernel(count, lists, rates, plan, reals):
    rep = lax.axis_index("rep")
    lanes = lists.shape[1]
    table = lists[0:8, :] + lists[8:16, :] + lists[16:24, :] + lists[24:32, :]
    home, other = table[0:1, :], table[1:2, :]
    valid = jnp.where(iota((1, lanes), 1) < 4 * count, 1, 0)
    ahead = ones_where(iota((lanes, lanes), 0) < iota((lanes, lanes), 1))

    def before(masks):
        part = iota((16, lanes), 0) // 4
        rows = masks[3]
        for n in range(3):
            rows = jnp.where(part == n, masks[n], rows)
        found = dot(rows.astype(F32).astype(BF16), ahead).astype(I32)
        return [found[4 * n : 4 * n + 1, :] for n in range(4)]

    def total(x):
        return jnp.sum(x.astype(F32), axis=1, keepdims=True).astype(I32)

    local = jnp.where(other < 2, valid, 0)
    start = jnp.zeros((1, 1), I32)
    quota = jnp.zeros((1, 1), I32)
    for q in range(4):
        room = jnp.maximum(count - total(jnp.where(other == 2 + q, valid, 0)), 0)
        start = start + jnp.where(q < rep, room, 0)
        quota = quota + jnp.where(q == rep, room, 0)
    turn = before([local] * 4)[0]
    taken = jnp.where(turn >= start, local, 0) * jnp.where(turn < start + quota, 1, 0)
    came = jnp.where(other == 2 + rep, valid, 0)
    masks = [jnp.where(home == t, x, 0) for x in (came, taken) for t in range(2)]
    place = jnp.full((1, lanes), -1, I32)
    ends = [jnp.zeros((1, 1), I32)]
    for mask, turn in zip(masks, before(masks)):
        place = jnp.where(mask > 0, turn + ends[-1] * QUAD, place)
        ends.append(ends[-1] + (total(mask) + (QUAD - 1)) // QUAD)
    put = ones_where(iota((lanes, lanes), 0) == place)
    row = iota((8, lanes), 0)
    fields = jnp.where(row == 1, jnp.minimum(table, 2), table)
    fields = jnp.where(row == 6, 1, fields).astype(F32)
    rate = jnp.zeros((1, lanes), F32)
    for k in range(rates.shape[0]):
        rate = jnp.where(table[2:3, :] == k, rates[k : k + 1, :], rate)
    parts = split3(rate)
    rate = jnp.zeros((8, lanes), F32)
    for n in range(3):
        rate = jnp.where(row == n, parts[n], rate)
    fields = jnp.concatenate([fields, rate], axis=0).astype(BF16)
    listed = dot(fields, put, NT)
    counts = listed[0:8, :].astype(I32)
    plan[...] = jnp.where(row == 3, ends[2], jnp.where(row == 4, ends[4], counts))
    rate = listed[8:9, :] + listed[9:10, :] + listed[10:11, :]
    empty = 1.0 - listed[6:7, :]
    reals[...] = jnp.where(row == 0, rate + empty, jnp.where(row == 7, empty * FAR, listed[0:8, :] * EDGE))


def halo_places(halo):
    side = halo[TILE : TILE + SIDE, :].astype(F32)
    return side[0:8, 0:TILE] + side[8:16, 0:TILE] + side[0:8, TILE : 2 * TILE]


def pair_fields(plan, reals, p):
    return plan[1, p], plan[2, p], reals[0, p], [reals[3 + c, p] for c in range(3)], reals[7, p]


def exponent_factors(block, rate, shift, away):
    at = [block[c : c + 1, :] + shift[c] for c in range(3)]
    at[0] = at[0] + away
    row = iota((8, TILE), 0)
    square = at[0] * at[0] + at[1] * at[1] + at[2] * at[2]
    factors = jnp.where(row == 0, -rate, jnp.where(row == 1, -rate * square, 0.0))
    for c in range(3):
        factors = jnp.where(row == 2 + c, at[c] * (2.0 * rate), factors)
    high, mid, low = split3(factors)
    return jnp.concatenate([high, high, high, mid, mid, low, low, mid], axis=0).astype(BF16)


def tile_terms(block, wide):
    at = [block[c : c + 1, :] for c in range(3)]
    row = iota((8, TILE), 0)
    factors = jnp.where(row == 0, at[0] * at[0] + at[1] * at[1] + at[2] * at[2], 0.0)
    factors = jnp.where(row == 1, 1.0, factors)
    for c in range(3):
        factors = jnp.where(row == 2 + c, at[c], factors)
    high, mid, low = split3(factors)
    for n, part in enumerate((high, mid, low, high, mid, high, mid, low)):
        wide[8 * n : 8 * n + 8, :] = part
    return jnp.transpose(wide[...]).astype(BF16)[:, 0:DEPTH]


def forward_groups(plan, reals, first, last, terms, places_of, mapped_of, message, held):
    def powers(q):
        terms_home = terms[plan[0, q * QUAD]]
        fields = [pair_fields(plan, reals, q * QUAD + u) for u in range(QUAD)]
        return [dot(terms_home, exponent_factors(places_of(f[0]), *f[2:])) for f in fields]

    def hold(found):
        for u in range(QUAD):
            held[:, u * TILE : (u + 1) * TILE] = jnp.exp(found[u]).astype(BF16)

    def products(q):
        at = q * QUAD
        across = [mapped_of(plan[2, at + u], plan[1, at + u]) for u in range(QUAD)]
        message[plan[0, at]] += dot(held[...], jnp.concatenate(across, axis=0))

    def step(q, carry):
        found = powers(q)
        products(q - 1)
        hold(found)
        return carry

    @pl.when(last > first)
    def _():
        hold(powers(first))
        lax.fori_loop(first + 1, last, step, 0)
        products(last - 1)


def home_forward_kernel(
    hbm_plan, hbm_reals, home_places, home_terms, radial, feat,
    home_mapped, message,
    plan, reals, held, sems,
):
    copies = fetch((hbm_plan, hbm_reals), (plan, reals), sems)
    for k in range(radial.shape[0]):
        home_mapped[k] = dot(feat[...], radial[k]).astype(BF16)
    message[...] = jnp.zeros_like(message)
    for copy in copies:
        copy.wait()
    forward_groups(
        plan, reals, plan[3, 0], plan[4, 0], home_terms,
        lambda slot: home_places[slot],
        lambda kind, slot: home_mapped[kind, tile_of(slot), :],
        message, held,
    )


def halo_forward_kernel(
    hbm_plan, hbm_reals, halo, home_places, home_terms, radial, home_message,
    mapped, places, terms, partial,
    plan, reals, wide, message, held, sems,
):
    copies = fetch((hbm_plan, hbm_reals), (plan, reals), sems)
    places[0:2] = home_places[...]
    places[2] = halo_places(halo)
    terms[0:2] = home_terms[...]
    wide[...] = jnp.zeros_like(wide)
    terms[2] = tile_terms(places[2], wide)
    for k in range(radial.shape[0]):
        mapped[k] = dot(halo[0:TILE, :], radial[k]).astype(BF16)
    message[...] = home_message[...]
    for copy in copies:
        copy.wait()
    forward_groups(
        plan, reals, 0, plan[3, 0], home_terms,
        lambda slot: places[2],
        lambda kind, slot: mapped[kind],
        message, held,
    )
    atoms = 2 * TILE
    for t in range(2):
        low = message[t].astype(BF16)
        for q in range(4):
            partial[q * atoms + t * TILE : q * atoms + (t + 1) * TILE, :] = low


def tile_of(slot):
    return pl.ds(pl.multiple_of(slot * TILE, TILE), TILE)


def marks(*which):
    row = iota((SIDE, TILE), 0)
    found = jnp.zeros((SIDE, TILE), F32)
    for r in which:
        found = jnp.where(row == r, 1.0, found)
    return found


def tile_sums(found, block, side):
    found = found[0:SIDE] + found[SIDE : 2 * SIDE]
    at = [block[c : c + 1, :] for c in range(3)]
    zeroth = found[0:1, :]
    once = [found[1 + c : 2 + c, :] for c in range(3)]
    side[...] = jnp.zeros_like(side)
    for c in range(3):
        side[c : c + 1, :] = once[c] - at[c] * zeroth
    for n, (a, b) in enumerate(COMPONENT_PAIRS):
        at_row = 4 + n if n < 3 else 5 + n
        twice = found[at_row : at_row + 1, :]
        side[8 + n : 9 + n, :] = -0.5 * (twice - at[b] * once[a] - at[a] * once[b] + at[a] * at[b] * zeroth)


def atom_kernel(partial, mixing, readout, adjoint, flipped, mixing_part):
    rep = lax.axis_index("rep")
    channels = mixing.shape[0]
    atoms = 2 * TILE
    message = partial[0:atoms, :].astype(F32)
    for q in range(1, 4):
        message = message + partial[q * atoms : (q + 1) * atoms, :].astype(F32)
    packed = message.astype(BF16)
    mixed = dot(packed, mixing[...])
    gate = jax.nn.sigmoid(mixed)
    slope = (readout[...] * gate * (1.0 + mixed * (1.0 - gate))).astype(BF16)
    adjoint[...] = dot(slope, mixing[...], NT).astype(BF16)
    for t in range(2):
        flipped[t] = dot(mixing[...], slope[t * TILE : (t + 1) * TILE, :], NT).astype(BF16)
    half = channels // 2
    share = channels // 4
    gradient = None
    for odd in range(2):
        take_rows = ones_where(iota((half, channels), 1) == 2 * iota((half, channels), 0) + odd)
        lane = iota((channels, TILE), 1) - odd * share
        inside = jnp.where(lane >= 0, 1, 0) * jnp.where(lane < share, 1, 0)
        take_cols = ones_where(jnp.where(inside > 0, lane + rep * share, -1) == iota((channels, TILE), 0))
        left = dot(take_rows, packed, NT).astype(BF16)
        right = dot(slope, take_cols).astype(BF16)
        part = dot(left, right)
        gradient = part if gradient is None else gradient + part
    mixing_part[...] = gradient


def tile_bases(block):
    left, right = marks(0), marks(0, 1, 2, 3)
    for c in range(3):
        left = left + LEFT_MARKS[c]() * block[c : c + 1, :]
        right = right + RIGHT_MARKS[c]() * block[c : c + 1, :]
    return jnp.concatenate([left, right], axis=0)


LEFT_MARKS = tuple(functools.partial(marks, *x) for x in ((1, 4, 8, 9), (2, 5, 10), (3, 6)))
RIGHT_MARKS = tuple(functools.partial(marks, *x) for x in ((4,), (5, 8), (6, 9, 10)))


def backward_groups(
    plan, reals, first, last, flipped, places, terms, spread, bases, mapped_of, tile_at, grads, sums, held, weights
):
    left_marks = [f() for f in LEFT_MARKS]
    right_marks = [f() for f in RIGHT_MARKS]

    def monomials(t, left_shift, right_shift):
        base = bases[t]
        high, low = split((base[0:SIDE] + left_shift) * (base[SIDE : 2 * SIDE] + right_shift))
        both = jnp.concatenate([high, low], axis=0).astype(BF16)
        return jnp.concatenate([both, both], axis=1)

    def begin(q):
        at = q * QUAD
        home = plan[0, at]
        fields = [pair_fields(plan, reals, at + u) for u in range(QUAD)]
        tiles = [mapped_of(kind, slot) for slot, kind, *_ in fields]
        pulls = dot(jnp.concatenate(tiles, axis=0), flipped[home])
        block = places[home]
        powers = [
            dot(terms[slot], exponent_factors(block, rate, [-x for x in shift], away))
            for slot, _, rate, shift, away in fields
        ]
        return [(powers[u], pulls[u * TILE : (u + 1) * TILE], fields[u][2]) for u in range(QUAD)]

    def hold(u, power, pull, rate):
        kernel = jnp.exp(power)
        held[u] = kernel.astype(BF16)
        weight = (kernel * (-2.0 * rate)) * pull
        high = weight.astype(BF16)
        weights[u, 0] = high
        weights[u, 1] = (weight - high.astype(F32)).astype(BF16)

    def finish(q, u):
        home = plan[0, q * QUAD]
        slot, kind, _, shift, _ = pair_fields(plan, reals, q * QUAD + u)
        left_shift = sum(left_marks[c] * shift[c] for c in range(3))
        right_shift = sum(right_marks[c] * shift[c] for c in range(3))
        far = monomials(slot, left_shift, right_shift)
        near = monomials(home, -left_shift, -right_shift)
        high, low = weights[u, 0], weights[u, 1]
        sums[slot] += dot(near, jnp.concatenate([high, low], axis=1), NT)
        grads[tile_at(slot), :] += dot(held[u], spread[kind, tile_of(home), :])
        return dot(far, jnp.concatenate([high, low], axis=0))

    def step(q, carry):
        found = begin(q)
        parts = []
        for u in range(QUAD):
            parts.append(finish(q - 1, u))
            hold(u, *found[u])
        sums[plan[0, (q - 1) * QUAD]] += sum(parts[1:], parts[0])
        return carry

    @pl.when(last > first)
    def _():
        for u, found in enumerate(begin(first)):
            hold(u, *found)
        lax.fori_loop(first + 1, last, step, 0)
        parts = [finish(last - 1, u) for u in range(QUAD)]
        sums[plan[0, (last - 1) * QUAD]] += sum(parts[1:], parts[0])


def halo_backward_kernel(
    hbm_plan, hbm_reals, adjoint, flipped, places, terms, radial, mapped,
    back, spread, bases, home_sums,
    plan, reals, grads, sums, side, held, weights, sems,
):
    copies = fetch((hbm_plan, hbm_reals), (plan, reals), sems)
    for k in range(radial.shape[0]):
        spread[k] = dot(adjoint[...], radial[k], NT).astype(BF16)
    for t in range(SLOTS):
        bases[t] = tile_bases(places[t])
    sums[...] = jnp.zeros_like(sums)
    grads[...] = jnp.zeros_like(grads)
    for copy in copies:
        copy.wait()
    backward_groups(
        plan, reals, 0, plan[3, 0], flipped, places, terms, spread, bases,
        lambda kind, slot: mapped[kind],
        lambda slot: slice(0, TILE),
        grads, sums, held, weights,
    )
    back[0:TILE, :] = grads[...].astype(BF16)
    tile_sums(sums[2], places[2], side)
    high, low = split(side[...])
    back[TILE : TILE + SIDE, 0:TILE] = high.astype(BF16)
    back[TILE : TILE + SIDE, TILE : 2 * TILE] = low.astype(BF16)
    home_sums[...] = sums[0:2]


def home_backward_kernel(
    hbm_plan, hbm_reals, flipped, places, terms, home_mapped, spread, bases, home_sums,
    own_grad, own_side,
    plan, reals, sums, side, held, weights, sems,
):
    copies = fetch((hbm_plan, hbm_reals), (plan, reals), sems)
    sums[...] = home_sums[...]
    own_grad[...] = jnp.zeros_like(own_grad)
    for copy in copies:
        copy.wait()
    backward_groups(
        plan, reals, plan[3, 0], plan[4, 0], flipped, places, terms, spread, bases,
        lambda kind, slot: home_mapped[kind, tile_of(slot), :],
        tile_of,
        own_grad, sums, held, weights,
    )
    for t in range(2):
        tile_sums(sums[t], places[t], side)
        own_side[:, t * TILE : (t + 1) * TILE] = side[...]


def return_kernel(rows, got, own_grad, own_side, payload):
    rep = lax.axis_index("rep")
    atoms = own_grad.shape[0]
    pick = ones_where(iota((atoms, TILE), 0) == rows[pl.ds(rep, 1), :])
    grad = (own_grad[...] + dot(pick, got[0:TILE, :])).astype(BF16)
    came = got[TILE : TILE + SIDE, :]
    side = own_side[...] + dot(came[:, 0:TILE], pick, NT) + dot(came[:, TILE : 2 * TILE], pick, NT)
    high, low = split(side)
    both = jnp.concatenate([high, low], axis=0).astype(BF16)
    height = atoms + 2 * SIDE
    for q in range(4):
        payload[q * height : q * height + atoms, :] = grad
        payload[q * height + atoms : (q + 1) * height, :] = both


def final_kernel(payload, mixing_parts, grad, forces, virials, grad_mixing):
    atoms = grad.shape[0]
    height = atoms + 2 * SIDE
    total = None
    side = None
    for q in range(4):
        part = payload[q * height : q * height + atoms, :].astype(F32)
        total = part if total is None else total + part
        both = payload[q * height + atoms : (q + 1) * height, :].astype(F32)
        part = both[0:SIDE] + both[SIDE : 2 * SIDE]
        side = part if side is None else side + part
    grad[...] = total.astype(BF16)
    forces[...] = side[0:3]
    virials[...] = side[8:14]
    found = jnp.sum(mixing_parts[...], axis=0, keepdims=True)
    share = grad_mixing.shape[1]
    grad_mixing[0:1, :] = found[:, 0:share]
    grad_mixing[1:2, :] = found[:, share : 2 * share]


def call(kernel, outs, ins, scratch=(), hbm=0, sems=0, away=(), flops=0, moved=1 << 20, limit=32 << 20):
    vmem = pl.BlockSpec(memory_space=pltpu.VMEM)
    stay = pl.BlockSpec(memory_space=pl.ANY)
    return pl.pallas_call(
        kernel,
        out_shape=[jax.ShapeDtypeStruct(shape, dtype) for shape, dtype in outs],
        in_specs=[stay if n < hbm or n in away else vmem for n in range(len(ins))],
        out_specs=[vmem] * len(outs),
        scratch_shapes=list(scratch) + ([pltpu.SemaphoreType.DMA((sems,))] if sems else []),
        compiler_params=pltpu.CompilerParams(vmem_limit_bytes=limit),
        cost_estimate=pl.CostEstimate(flops=flops, bytes_accessed=moved, transcendentals=0),
    )(*ins)


def on_device(
    features, positions, radial, mixing, readout, decay,
    send_rows, pair_home, pair_other, pair_kind, pair_image,
):
    atoms, channels = features.shape
    kinds = radial.shape[0]
    count = pair_home.shape[0]
    doms, reps = lax.axis_size("dom"), lax.axis_size("rep")
    lanes = 2 * TILE
    height = atoms + 2 * SIDE
    assert reps == len(OFFSETS) and atoms == 2 * TILE and 4 * count + 4 * QUAD <= lanes
    assert channels == 2 * doms

    def hop(array, sign):
        ways = [
            (d * reps + r, (d + sign * OFFSETS[r]) % doms * reps + r)
            for d in range(doms)
            for r in range(reps)
        ]
        return lax.ppermute(array, ("dom", "rep"), ways)

    def swap(array, axis):
        return lax.all_to_all(array, axis, 0, 0, tiled=True)

    vmem, smem = pltpu.VMEM, pltpu.SMEM
    sent = [send_rows, *(x.reshape(1, count) for x in (pair_home, pair_other, pair_kind))]
    sent += [pair_image, positions, features]
    send, lists = call(
        pack_kernel,
        [((TILE + SIDE, channels), BF16), ((32, lanes), I32)],
        sent,
        [vmem(x.shape, x.dtype) for x in sent[:5]]
        + [vmem((8, atoms), F32), vmem(features.shape, BF16), vmem((8, lanes), I32)],
        hbm=len(sent),
        sems=len(sent),
        flops=1 << 30,
        limit=63 << 20,
    )
    halo = hop(send, 1)
    lists = swap(lists, "rep")
    rates, home_places, home_terms, readout, send_rows = call(
        local_kernel,
        [
            ((kinds, lanes), F32),
            ((2, 8, TILE), F32),
            ((2, TILE, DEPTH), BF16),
            ((1, channels), F32),
            (send_rows.shape, I32),
        ],
        [decay, readout.reshape(1, channels), send_rows, positions],
        [smem(decay.shape, F32), vmem((TILE, TILE), F32)],
        hbm=3,
        sems=3,
        flops=1 << 32,
    )
    plan, reals = call(
        functools.partial(plan_kernel, count),
        [((8, lanes), I32), ((8, lanes), F32)],
        [lists, rates],
        flops=1 << 20,
    )
    tables = [smem((8, lanes), I32), smem((8, lanes), F32)]
    home_mapped, message = call(
        home_forward_kernel,
        [((kinds, atoms, channels), BF16), ((2, TILE, channels), F32)],
        [plan, reals, home_places, home_terms, radial, features],
        tables + [vmem((TILE, QUAD * TILE), BF16)],
        hbm=2,
        sems=2,
        flops=1 << 32,
    )
    mapped, places, terms, partial = call(
        halo_forward_kernel,
        [
            ((kinds, TILE, channels), BF16),
            ((SLOTS, 8, TILE), F32),
            ((SLOTS, TILE, DEPTH), BF16),
            ((reps * atoms, channels), BF16),
        ],
        [plan, reals, halo, home_places, home_terms, radial, message],
        tables
        + [vmem((TILE, TILE), F32), vmem((2, TILE, channels), F32), vmem((TILE, QUAD * TILE), BF16)],
        hbm=2,
        sems=2,
        flops=1 << 31,
    )
    partial = swap(partial, "rep")
    adjoint, flipped, mixing_part = call(
        atom_kernel,
        [((atoms, channels), BF16), ((2, channels, TILE), BF16), ((channels // 2, TILE), F32)],
        [partial, mixing, readout],
        flops=1 << 28,
    )
    mixing_parts = swap(mixing_part, "dom")
    group_space = [vmem((SIDE, TILE), F32), vmem((QUAD, TILE, TILE), BF16), vmem((QUAD, 2, TILE, TILE), BF16)]
    back, spread, bases, home_sums = call(
        halo_backward_kernel,
        [
            ((TILE + SIDE, channels), BF16),
            ((kinds, atoms, channels), BF16),
            ((SLOTS, 2 * SIDE, TILE), F32),
            ((2, 2 * SIDE, TILE), F32),
        ],
        [plan, reals, adjoint, flipped, places, terms, radial, mapped],
        tables + [vmem((TILE, channels), F32), vmem((SLOTS, 2 * SIDE, TILE), F32)] + group_space,
        hbm=2,
        sems=2,
        flops=1 << 33,
    )
    got = hop(back, -1)
    own_grad, own_side = call(
        home_backward_kernel,
        [((atoms, channels), F32), ((SIDE, atoms), F32)],
        [plan, reals, flipped, places, terms, home_mapped, spread, bases, home_sums],
        tables + [vmem((2, 2 * SIDE, TILE), F32)] + group_space,
        hbm=2,
        sems=2,
        flops=1 << 32,
    )
    [payload] = call(
        return_kernel,
        [((reps * height, channels), BF16)],
        [send_rows, got, own_grad, own_side],
        flops=1 << 24,
    )
    payload = swap(payload, "rep")
    return tuple(
        call(
            final_kernel,
            [((atoms, channels), BF16), ((3, atoms), F32), ((6, atoms), F32), ((2, channels // reps), F32)],
            [payload, mixing_parts],
        )
    )


def solution(mesh):
    in_specs = (
        P("dom", None),
        P(None, "dom"),
        P(),
        P(),
        P(),
        P(),
        P(None, "dom"),
        P(("dom", "rep")),
        P(("dom", "rep")),
        P(("dom", "rep")),
        P(None, ("dom", "rep")),
    )
    out_specs = (P("dom", None), P(None, "dom"), P(None, "dom"), P("dom", "rep"))
    return jax.shard_map(
        on_device, mesh=mesh, in_specs=in_specs, out_specs=out_specs, check_vma=False
    )
```

```python
import functools

import jax
import jax.numpy as jnp
from jax import lax
from jax.experimental import pallas as pl
from jax.experimental.pallas import tpu as pltpu
from jax.sharding import PartitionSpec as P

TILE = 128
SLOTS = 3
QUAD = 8
SIDE = 16
OFFSETS = (1, -1, 2, -2)
EDGE = 2.0
FAR = 1.0e4
DEPTH = 64
F32, BF16, I32 = jnp.float32, jnp.bfloat16, jnp.int32
COMPONENT_PAIRS = ((0, 0), (1, 1), (2, 2), (0, 1), (0, 2), (1, 2))

NN = (((1,), (0,)), ((), ()))
NT = (((1,), (1,)), ((), ()))
TN = (((0,), (0,)), ((), ()))


def dot(a, b, dims=NN):
    return lax.dot_general(a, b, dims, preferred_element_type=F32)


def iota(shape, dim):
    return lax.broadcasted_iota(I32, shape, dim)


def ones_where(mask, dtype=BF16):
    return jnp.where(mask, 1.0, 0.0).astype(dtype)


def split(x):
    high = x.astype(BF16).astype(F32)
    return high, (x - high).astype(BF16).astype(F32)


def split3(x):
    high, mid = split(x)
    return high, mid, x - high - mid


def fetch(sources, targets, sems):
    copies = [pltpu.make_async_copy(a, b, sems.at[n]) for n, (a, b) in enumerate(zip(sources, targets))]
    for copy in copies:
        copy.start()
    return copies


def pack_kernel(
    hbm_rows, hbm_home, hbm_other, hbm_kind, hbm_image, hbm_pos, hbm_feat,
    send, lists,
    rows, home, other, kind, image, pos, feat, block, sems,
):
    copies = fetch(
        (hbm_rows, hbm_home, hbm_other, hbm_kind, hbm_image, hbm_pos, hbm_feat),
        (rows, home, other, kind, image, pos.at[0:3, :], feat),
        sems,
    )
    rep = lax.axis_index("rep")
    atoms = feat.shape[0]
    count = home.shape[1]
    pos[3:8, :] = jnp.zeros((5, atoms), F32)
    block[...] = jnp.zeros_like(block)
    for copy in copies:
        copy.wait()
    pick = ones_where(iota((atoms, TILE), 0) == rows[pl.ds(rep, 1), :])
    send[0:TILE, :] = dot(pick, feat[...], TN).astype(BF16)
    parts = jnp.concatenate([*split3(pos[...]), jnp.zeros_like(pos)], axis=0).astype(BF16)
    moved = dot(parts, pick).astype(BF16)
    send[TILE : TILE + SIDE, 0:TILE] = moved[0:SIDE]
    send[TILE : TILE + SIDE, TILE : 2 * TILE] = moved[SIDE : 2 * SIDE]
    for q in range(4):

        @pl.when(rep == q)
        def _(q=q):
            span = slice(q * count, (q + 1) * count)
            block[0:1, span] = home[...]
            block[1:2, span] = other[...]
            block[2:3, span] = kind[...]
            block[3:6, span] = image[...]

    for q in range(4):
        lists[8 * q : 8 * q + 8, :] = block[...]


def local_kernel(
    hbm_decay, hbm_readout, hbm_rows, pos,
    rates, places, terms, readout, rows,
    decay, wide, sems,
):
    copy, *later = fetch([hbm_decay, hbm_readout, hbm_rows], [decay, readout, rows], sems)
    places[...] = jnp.zeros_like(places)
    wide[...] = jnp.zeros_like(wide)
    copy.wait()
    for k in range(rates.shape[0]):
        rates[k : k + 1, :] = jnp.full((1, rates.shape[1]), decay[k], F32)
    for t in range(2):
        places[t, 0:3, :] = pos[:, t * TILE : (t + 1) * TILE]
        terms[t] = tile_terms(places[t], wide)
    for copy in later:
        copy.wait()


def plan_kernel(count, lists, rates, plan, reals):
    rep = lax.axis_index("rep")
    lanes = lists.shape[1]
    table = lists[0:8, :] + lists[8:16, :] + lists[16:24, :] + lists[24:32, :]
    home, other = table[0:1, :], table[1:2, :]
    valid = jnp.where(iota((1, lanes), 1) < 4 * count, 1, 0)
    ahead = ones_where(iota((lanes, lanes), 0) < iota((lanes, lanes), 1))

    def before(masks):
        part = iota((16, lanes), 0) // 4
        rows = masks[3]
        for n in range(3):
            rows = jnp.where(part == n, masks[n], rows)
        found = dot(rows.astype(F32).astype(BF16), ahead).astype(I32)
        return [found[4 * n : 4 * n + 1, :] for n in range(4)]

    def total(x):
        return jnp.sum(x.astype(F32), axis=1, keepdims=True).astype(I32)

    local = jnp.where(other < 2, valid, 0)
    start = jnp.zeros((1, 1), I32)
    quota = jnp.zeros((1, 1), I32)
    for q in range(4):
        room = jnp.maximum(count - total(jnp.where(other == 2 + q, valid, 0)), 0)
        start = start + jnp.where(q < rep, room, 0)
        quota = quota + jnp.where(q == rep, room, 0)
    turn = before([local] * 4)[0]
    taken = jnp.where(turn >= start, local, 0) * jnp.where(turn < start + quota, 1, 0)
    came = jnp.where(other == 2 + rep, valid, 0)
    masks = [jnp.where(home == t, x, 0) for x in (came, taken) for t in range(2)]
    place = jnp.full((1, lanes), -1, I32)
    ends = [jnp.zeros((1, 1), I32)]
    for mask, turn in zip(masks, before(masks)):
        place = jnp.where(mask > 0, turn + ends[-1] * QUAD, place)
        ends.append(ends[-1] + (total(mask) + (QUAD - 1)) // QUAD)
    put = ones_where(iota((lanes, lanes), 0) == place)
    row = iota((8, lanes), 0)
    fields = jnp.where(row == 1, jnp.minimum(table, 2), table)
    fields = jnp.where(row == 6, 1, fields).astype(F32)
    rate = jnp.zeros((1, lanes), F32)
    for k in range(rates.shape[0]):
        rate = jnp.where(table[2:3, :] == k, rates[k : k + 1, :], rate)
    parts = split3(rate)
    rate = jnp.zeros((8, lanes), F32)
    for n in range(3):
        rate = jnp.where(row == n, parts[n], rate)
    fields = jnp.concatenate([fields, rate], axis=0).astype(BF16)
    listed = dot(fields, put, NT)
    counts = listed[0:8, :].astype(I32)
    plan[...] = jnp.where(row == 3, ends[2], jnp.where(row == 4, ends[4], counts))
    rate = listed[8:9, :] + listed[9:10, :] + listed[10:11, :]
    empty = 1.0 - listed[6:7, :]
    reals[...] = jnp.where(row == 0, rate + empty, jnp.where(row == 7, empty * FAR, listed[0:8, :] * EDGE))


def halo_places(halo):
    side = halo[TILE : TILE + SIDE, :].astype(F32)
    return side[0:8, 0:TILE] + side[8:16, 0:TILE] + side[0:8, TILE : 2 * TILE]


def pair_fields(plan, reals, p):
    return plan[1, p], plan[2, p], reals[0, p], [reals[3 + c, p] for c in range(3)], reals[7, p]


def exponent_factors(block, rate, shift, away):
    at = [block[c : c + 1, :] + shift[c] for c in range(3)]
    at[0] = at[0] + away
    row = iota((8, TILE), 0)
    square = at[0] * at[0] + at[1] * at[1] + at[2] * at[2]
    factors = jnp.where(row == 0, -rate, jnp.where(row == 1, -rate * square, 0.0))
    for c in range(3):
        factors = jnp.where(row == 2 + c, at[c] * (2.0 * rate), factors)
    high, mid, low = split3(factors)
    return jnp.concatenate([high, high, high, mid, mid, low, low, mid], axis=0).astype(BF16)


def tile_terms(block, wide):
    at = [block[c : c + 1, :] for c in range(3)]
    row = iota((8, TILE), 0)
    factors = jnp.where(row == 0, at[0] * at[0] + at[1] * at[1] + at[2] * at[2], 0.0)
    factors = jnp.where(row == 1, 1.0, factors)
    for c in range(3):
        factors = jnp.where(row == 2 + c, at[c], factors)
    high, mid, low = split3(factors)
    for n, part in enumerate((high, mid, low, high, mid, high, mid, low)):
        wide[8 * n : 8 * n + 8, :] = part
    return jnp.transpose(wide[...]).astype(BF16)[:, 0:DEPTH]


def forward_groups(plan, reals, first, last, terms, places_of, mapped_of, message, held):
    def powers(q):
        terms_home = terms[plan[0, q * QUAD]]
        fields = [pair_fields(plan, reals, q * QUAD + u) for u in range(QUAD)]
        return [dot(terms_home, exponent_factors(places_of(f[0]), *f[2:])) for f in fields]

    def hold(found):
        for u in range(QUAD):
            held[:, u * TILE : (u + 1) * TILE] = jnp.exp(found[u]).astype(BF16)

    def products(q):
        at = q * QUAD
        across = [mapped_of(plan[2, at + u], plan[1, at + u]) for u in range(QUAD)]
        message[plan[0, at]] += dot(held[...], jnp.concatenate(across, axis=0))

    def step(q, carry):
        found = powers(q)
        products(q - 1)
        hold(found)
        return carry

    @pl.when(last > first)
    def _():
        hold(powers(first))
        lax.fori_loop(first + 1, last, step, 0)
        products(last - 1)


def home_forward_kernel(
    hbm_plan, hbm_reals, home_places, home_terms, radial, feat,
    home_mapped, message,
    plan, reals, held, sems,
):
    copies = fetch((hbm_plan, hbm_reals), (plan, reals), sems)
    for k in range(radial.shape[0]):
        home_mapped[k] = dot(feat[...], radial[k]).astype(BF16)
    message[...] = jnp.zeros_like(message)
    for copy in copies:
        copy.wait()
    forward_groups(
        plan, reals, plan[3, 0], plan[4, 0], home_terms,
        lambda slot: home_places[slot],
        lambda kind, slot: home_mapped[kind, tile_of(slot), :],
        message, held,
    )


def halo_forward_kernel(
    hbm_plan, hbm_reals, halo, home_places, home_terms, radial, home_message,
    mapped, places, terms, partial,
    plan, reals, wide, message, held, sems,
):
    copies = fetch((hbm_plan, hbm_reals), (plan, reals), sems)
    places[0:2] = home_places[...]
    places[2] = halo_places(halo)
    terms[0:2] = home_terms[...]
    wide[...] = jnp.zeros_like(wide)
    terms[2] = tile_terms(places[2], wide)
    for k in range(radial.shape[0]):
        mapped[k] = dot(halo[0:TILE, :], radial[k]).astype(BF16)
    message[...] = home_message[...]
    for copy in copies:
        copy.wait()
    forward_groups(
        plan, reals, 0, plan[3, 0], home_terms,
        lambda slot: places[2],
        lambda kind, slot: mapped[kind],
        message, held,
    )
    atoms = 2 * TILE
    for t in range(2):
        low = message[t].astype(BF16)
        for q in range(4):
            partial[q * atoms + t * TILE : q * atoms + (t + 1) * TILE, :] = low


def tile_of(slot):
    return pl.ds(pl.multiple_of(slot * TILE, TILE), TILE)


def marks(*which):
    row = iota((SIDE, TILE), 0)
    found = jnp.zeros((SIDE, TILE), F32)
    for r in which:
        found = jnp.where(row == r, 1.0, found)
    return found


def tile_sums(found, block, side):
    found = found[0:SIDE] + found[SIDE : 2 * SIDE]
    at = [block[c : c + 1, :] for c in range(3)]
    zeroth = found[0:1, :]
    once = [found[1 + c : 2 + c, :] for c in range(3)]
    side[...] = jnp.zeros_like(side)
    for c in range(3):
        side[c : c + 1, :] = once[c] - at[c] * zeroth
    for n, (a, b) in enumerate(COMPONENT_PAIRS):
        at_row = 4 + n if n < 3 else 5 + n
        twice = found[at_row : at_row + 1, :]
        side[8 + n : 9 + n, :] = -0.5 * (twice - at[b] * once[a] - at[a] * once[b] + at[a] * at[b] * zeroth)


def atom_kernel(partial, mixing, readout, adjoint, flipped, mixing_part):
    rep = lax.axis_index("rep")
    channels = mixing.shape[0]
    atoms = 2 * TILE
    message = partial[0:atoms, :].astype(F32)
    for q in range(1, 4):
        message = message + partial[q * atoms : (q + 1) * atoms, :].astype(F32)
    packed = message.astype(BF16)
    mixed = dot(packed, mixing[...])
    gate = jax.nn.sigmoid(mixed)
    slope = (readout[...] * gate * (1.0 + mixed * (1.0 - gate))).astype(BF16)
    adjoint[...] = dot(slope, mixing[...], NT).astype(BF16)
    for t in range(2):
        flipped[t] = dot(mixing[...], slope[t * TILE : (t + 1) * TILE, :], NT).astype(BF16)
    half = channels // 2
    share = channels // 4
    gradient = None
    for odd in range(2):
        take_rows = ones_where(iota((half, channels), 1) == 2 * iota((half, channels), 0) + odd)
        lane = iota((channels, TILE), 1) - odd * share
        inside = jnp.where(lane >= 0, 1, 0) * jnp.where(lane < share, 1, 0)
        take_cols = ones_where(jnp.where(inside > 0, lane + rep * share, -1) == iota((channels, TILE), 0))
        left = dot(take_rows, packed, NT).astype(BF16)
        right = dot(slope, take_cols).astype(BF16)
        part = dot(left, right)
        gradient = part if gradient is None else gradient + part
    mixing_part[...] = gradient


def tile_bases(block):
    left, right = marks(0), marks(0, 1, 2, 3)
    for c in range(3):
        left = left + LEFT_MARKS[c]() * block[c : c + 1, :]
        right = right + RIGHT_MARKS[c]() * block[c : c + 1, :]
    return jnp.concatenate([left, right], axis=0)


LEFT_MARKS = tuple(functools.partial(marks, *x) for x in ((1, 4, 8, 9), (2, 5, 10), (3, 6)))
RIGHT_MARKS = tuple(functools.partial(marks, *x) for x in ((4,), (5, 8), (6, 9, 10)))


def backward_groups(
    plan, reals, first, last, flipped, places, terms, spread, bases, mapped_of, tile_at, grads, sums, held, weights
):
    left_marks = [f() for f in LEFT_MARKS]
    right_marks = [f() for f in RIGHT_MARKS]

    def monomials(t, left_shift, right_shift):
        base = bases[t]
        high, low = split((base[0:SIDE] + left_shift) * (base[SIDE : 2 * SIDE] + right_shift))
        both = jnp.concatenate([high, low], axis=0).astype(BF16)
        return jnp.concatenate([both, both], axis=1)

    def begin(q):
        at = q * QUAD
        home = plan[0, at]
        fields = [pair_fields(plan, reals, at + u) for u in range(QUAD)]
        tiles = [mapped_of(kind, slot) for slot, kind, *_ in fields]
        pulls = dot(jnp.concatenate(tiles, axis=0), flipped[home])
        block = places[home]
        powers = [
            dot(terms[slot], exponent_factors(block, rate, [-x for x in shift], away))
            for slot, _, rate, shift, away in fields
        ]
        return [(powers[u], pulls[u * TILE : (u + 1) * TILE], fields[u][2]) for u in range(QUAD)]

    def hold(u, power, pull, rate):
        kernel = jnp.exp(power)
        held[u] = kernel.astype(BF16)
        weight = (kernel * (-2.0 * rate)) * pull
        high = weight.astype(BF16)
        weights[u, 0] = high
        weights[u, 1] = (weight - high.astype(F32)).astype(BF16)

    def gather(q):
        if tile_at is None:
            home = tile_of(plan[0, q * QUAD])
            across = [spread[plan[2, q * QUAD + u], home, :] for u in range(QUAD)]
            kernels = jnp.concatenate([held[u] for u in range(QUAD)], axis=1)
            grads[...] += dot(kernels, jnp.concatenate(across, axis=0))

    def finish(q, u):
        home = plan[0, q * QUAD]
        slot, kind, _, shift, _ = pair_fields(plan, reals, q * QUAD + u)
        left_shift = sum(left_marks[c] * shift[c] for c in range(3))
        right_shift = sum(right_marks[c] * shift[c] for c in range(3))
        far = monomials(slot, left_shift, right_shift)
        near = monomials(home, -left_shift, -right_shift)
        high, low = weights[u, 0], weights[u, 1]
        sums[slot] += dot(near, jnp.concatenate([high, low], axis=1), NT)
        if tile_at is not None:
            grads[tile_at(slot), :] += dot(held[u], spread[kind, tile_of(home), :])
        return dot(far, jnp.concatenate([high, low], axis=0))

    def step(q, carry):
        found = begin(q)
        gather(q - 1)
        parts = []
        for u in range(QUAD):
            parts.append(finish(q - 1, u))
            hold(u, *found[u])
        sums[plan[0, (q - 1) * QUAD]] += sum(parts[1:], parts[0])
        return carry

    @pl.when(last > first)
    def _():
        for u, found in enumerate(begin(first)):
            hold(u, *found)
        lax.fori_loop(first + 1, last, step, 0)
        gather(last - 1)
        parts = [finish(last - 1, u) for u in range(QUAD)]
        sums[plan[0, (last - 1) * QUAD]] += sum(parts[1:], parts[0])


def halo_backward_kernel(
    hbm_plan, hbm_reals, adjoint, flipped, places, terms, radial, mapped,
    back, spread, bases, home_sums,
    plan, reals, grads, sums, side, held, weights, sems,
):
    copies = fetch((hbm_plan, hbm_reals), (plan, reals), sems)
    for k in range(radial.shape[0]):
        spread[k] = dot(adjoint[...], radial[k], NT).astype(BF16)
    for t in range(SLOTS):
        bases[t] = tile_bases(places[t])
    sums[...] = jnp.zeros_like(sums)
    grads[...] = jnp.zeros_like(grads)
    for copy in copies:
        copy.wait()
    backward_groups(
        plan, reals, 0, plan[3, 0], flipped, places, terms, spread, bases,
        lambda kind, slot: mapped[kind],
        None,
        grads, sums, held, weights,
    )
    back[0:TILE, :] = grads[...].astype(BF16)
    tile_sums(sums[2], places[2], side)
    high, low = split(side[...])
    back[TILE : TILE + SIDE, 0:TILE] = high.astype(BF16)
    back[TILE : TILE + SIDE, TILE : 2 * TILE] = low.astype(BF16)
    home_sums[...] = sums[0:2]


def home_backward_kernel(
    hbm_plan, hbm_reals, flipped, places, terms, home_mapped, spread, bases, home_sums,
    own_grad, own_side,
    plan, reals, sums, side, held, weights, sems,
):
    copies = fetch((hbm_plan, hbm_reals), (plan, reals), sems)
    sums[...] = home_sums[...]
    own_grad[...] = jnp.zeros_like(own_grad)
    for copy in copies:
        copy.wait()
    backward_groups(
        plan, reals, plan[3, 0], plan[4, 0], flipped, places, terms, spread, bases,
        lambda kind, slot: home_mapped[kind, tile_of(slot), :],
        tile_of,
        own_grad, sums, held, weights,
    )
    for t in range(2):
        tile_sums(sums[t], places[t], side)
        own_side[:, t * TILE : (t + 1) * TILE] = side[...]


def return_kernel(rows, got, own_grad, own_side, payload):
    rep = lax.axis_index("rep")
    atoms = own_grad.shape[0]
    pick = ones_where(iota((atoms, TILE), 0) == rows[pl.ds(rep, 1), :])
    grad = (own_grad[...] + dot(pick, got[0:TILE, :])).astype(BF16)
    came = got[TILE : TILE + SIDE, :]
    side = own_side[...] + dot(came[:, 0:TILE], pick, NT) + dot(came[:, TILE : 2 * TILE], pick, NT)
    high, low = split(side)
    both = jnp.concatenate([high, low], axis=0).astype(BF16)
    height = atoms + 2 * SIDE
    for q in range(4):
        payload[q * height : q * height + atoms, :] = grad
        payload[q * height + atoms : (q + 1) * height, :] = both


def final_kernel(payload, mixing_parts, grad, forces, virials, grad_mixing):
    atoms = grad.shape[0]
    height = atoms + 2 * SIDE
    total = None
    side = None
    for q in range(4):
        part = payload[q * height : q * height + atoms, :].astype(F32)
        total = part if total is None else total + part
        both = payload[q * height + atoms : (q + 1) * height, :].astype(F32)
        part = both[0:SIDE] + both[SIDE : 2 * SIDE]
        side = part if side is None else side + part
    grad[...] = total.astype(BF16)
    forces[...] = side[0:3]
    virials[...] = side[8:14]
    found = jnp.sum(mixing_parts[...], axis=0, keepdims=True)
    share = grad_mixing.shape[1]
    grad_mixing[0:1, :] = found[:, 0:share]
    grad_mixing[1:2, :] = found[:, share : 2 * share]


def call(kernel, outs, ins, scratch=(), hbm=0, sems=0, away=(), flops=0, moved=1 << 20, limit=32 << 20):
    vmem = pl.BlockSpec(memory_space=pltpu.VMEM)
    stay = pl.BlockSpec(memory_space=pl.ANY)
    return pl.pallas_call(
        kernel,
        out_shape=[jax.ShapeDtypeStruct(shape, dtype) for shape, dtype in outs],
        in_specs=[stay if n < hbm or n in away else vmem for n in range(len(ins))],
        out_specs=[vmem] * len(outs),
        scratch_shapes=list(scratch) + ([pltpu.SemaphoreType.DMA((sems,))] if sems else []),
        compiler_params=pltpu.CompilerParams(vmem_limit_bytes=limit),
        cost_estimate=pl.CostEstimate(flops=flops, bytes_accessed=moved, transcendentals=0),
    )(*ins)


def on_device(
    features, positions, radial, mixing, readout, decay,
    send_rows, pair_home, pair_other, pair_kind, pair_image,
):
    atoms, channels = features.shape
    kinds = radial.shape[0]
    count = pair_home.shape[0]
    doms, reps = lax.axis_size("dom"), lax.axis_size("rep")
    lanes = 2 * TILE
    height = atoms + 2 * SIDE
    assert reps == len(OFFSETS) and atoms == 2 * TILE and 4 * count + 4 * QUAD <= lanes
    assert channels == 2 * doms

    def hop(array, sign):
        ways = [
            (d * reps + r, (d + sign * OFFSETS[r]) % doms * reps + r)
            for d in range(doms)
            for r in range(reps)
        ]
        return lax.ppermute(array, ("dom", "rep"), ways)

    def swap(array, axis):
        return lax.all_to_all(array, axis, 0, 0, tiled=True)

    vmem, smem = pltpu.VMEM, pltpu.SMEM
    sent = [send_rows, *(x.reshape(1, count) for x in (pair_home, pair_other, pair_kind))]
    sent += [pair_image, positions, features]
    send, lists = call(
        pack_kernel,
        [((TILE + SIDE, channels), BF16), ((32, lanes), I32)],
        sent,
        [vmem(x.shape, x.dtype) for x in sent[:5]]
        + [vmem((8, atoms), F32), vmem(features.shape, BF16), vmem((8, lanes), I32)],
        hbm=len(sent),
        sems=len(sent),
        flops=1 << 30,
        limit=63 << 20,
    )
    halo = hop(send, 1)
    lists = swap(lists, "rep")
    rates, home_places, home_terms, readout, send_rows = call(
        local_kernel,
        [
            ((kinds, lanes), F32),
            ((2, 8, TILE), F32),
            ((2, TILE, DEPTH), BF16),
            ((1, channels), F32),
            (send_rows.shape, I32),
        ],
        [decay, readout.reshape(1, channels), send_rows, positions],
        [smem(decay.shape, F32), vmem((TILE, TILE), F32)],
        hbm=3,
        sems=3,
        flops=1 << 32,
    )
    plan, reals = call(
        functools.partial(plan_kernel, count),
        [((8, lanes), I32), ((8, lanes), F32)],
        [lists, rates],
        flops=1 << 20,
    )
    tables = [smem((8, lanes), I32), smem((8, lanes), F32)]
    home_mapped, message = call(
        home_forward_kernel,
        [((kinds, atoms, channels), BF16), ((2, TILE, channels), F32)],
        [plan, reals, home_places, home_terms, radial, features],
        tables + [vmem((TILE, QUAD * TILE), BF16)],
        hbm=2,
        sems=2,
        flops=1 << 32,
    )
    mapped, places, terms, partial = call(
        halo_forward_kernel,
        [
            ((kinds, TILE, channels), BF16),
            ((SLOTS, 8, TILE), F32),
            ((SLOTS, TILE, DEPTH), BF16),
            ((reps * atoms, channels), BF16),
        ],
        [plan, reals, halo, home_places, home_terms, radial, message],
        tables
        + [vmem((TILE, TILE), F32), vmem((2, TILE, channels), F32), vmem((TILE, QUAD * TILE), BF16)],
        hbm=2,
        sems=2,
        flops=1 << 31,
    )
    partial = swap(partial, "rep")
    adjoint, flipped, mixing_part = call(
        atom_kernel,
        [((atoms, channels), BF16), ((2, channels, TILE), BF16), ((channels // 2, TILE), F32)],
        [partial, mixing, readout],
        flops=1 << 28,
    )
    mixing_parts = swap(mixing_part, "dom")
    group_space = [vmem((SIDE, TILE), F32), vmem((QUAD, TILE, TILE), BF16), vmem((QUAD, 2, TILE, TILE), BF16)]
    back, spread, bases, home_sums = call(
        halo_backward_kernel,
        [
            ((TILE + SIDE, channels), BF16),
            ((kinds, atoms, channels), BF16),
            ((SLOTS, 2 * SIDE, TILE), F32),
            ((2, 2 * SIDE, TILE), F32),
        ],
        [plan, reals, adjoint, flipped, places, terms, radial, mapped],
        tables + [vmem((TILE, channels), F32), vmem((SLOTS, 2 * SIDE, TILE), F32)] + group_space,
        hbm=2,
        sems=2,
        flops=1 << 33,
    )
    got = hop(back, -1)
    own_grad, own_side = call(
        home_backward_kernel,
        [((atoms, channels), F32), ((SIDE, atoms), F32)],
        [plan, reals, flipped, places, terms, home_mapped, spread, bases, home_sums],
        tables + [vmem((2, 2 * SIDE, TILE), F32)] + group_space,
        hbm=2,
        sems=2,
        flops=1 << 32,
    )
    [payload] = call(
        return_kernel,
        [((reps * height, channels), BF16)],
        [send_rows, got, own_grad, own_side],
        flops=1 << 24,
    )
    payload = swap(payload, "rep")
    return tuple(
        call(
            final_kernel,
            [((atoms, channels), BF16), ((3, atoms), F32), ((6, atoms), F32), ((2, channels // reps), F32)],
            [payload, mixing_parts],
        )
    )


def solution(mesh):
    in_specs = (
        P("dom", None),
        P(None, "dom"),
        P(),
        P(),
        P(),
        P(),
        P(None, "dom"),
        P(("dom", "rep")),
        P(("dom", "rep")),
        P(("dom", "rep")),
        P(None, ("dom", "rep")),
    )
    out_specs = (P("dom", None), P(None, "dom"), P(None, "dom"), P("dom", "rep"))
    return jax.shard_map(
        on_device, mesh=mesh, in_specs=in_specs, out_specs=out_specs, check_vma=False
    )
```
